512 devices in a mesh: row: 32 (over x_lo, z), col: 16 (over y, x_hi, core).
Axes of the slice: x: 4 (x_hi: 2, x_lo: 2; x = x_hi * 2 + x_lo), y: 4, z: 16, core: 2. Of those that a mesh axis runs over, the one named last changes fastest.
Arguments:
- activations: bfloat16 [4096, 8192], P('row', 'col'), may hold values from -6 to 6
- w_value: bfloat16 [8192, 4096], P('row', 'col'), may hold values from -0.125 to 0.125
- query_input: bfloat16 [4096, 4096], P('row', 'col'), may hold values from -6 to 6
- key_input: bfloat16 [4096, 4096], P('row', 'col'), may hold values from -6 to 6
- log_decay: float32 [32, 4096], P('col', 'row'), may hold values from -0.7 to 0, as said below
- write_rate: float32 [32, 4096], P('col', 'row'), may hold values from 0.02 to 0.2
- norm_gain: float32 [128], replicated, may hold values from 0.1 to 1.9
- out_grad: bfloat16 [4096, 4096], P('row', 'col'), may hold values from -6 to 6
Outputs:
- layer_out: bfloat16 [4096, 4096], P('row', 'col')
- d_input: bfloat16 [4096, 8192], P('row', 'col')
- d_query: bfloat16 [4096, 4096], P('row', 'col')
- d_key: bfloat16 [4096, 4096], P('row', 'col')
- d_w_value: float32 [8192, 4096], P('row', 'col')
The draws below stay inside these ranges and needn't reach their ends.
Inputs may be any that keep to these rules, and one draw needn't show every extreme that they name: log_decay is never positive.
All inputs are finite; a program needn't handle non-finite values.
Results may differ from the reference program's by a relative error of at most 0.025.
Values may be sent and summed in bfloat16 or wider, within the bound.
A program may use at most 64 MiB of HBM per device.

```python
import math
import jax
import jax.numpy as jnp
from jax import lax

D = 8192
LOCAL_HEADS = 32
DH = 128
TOK_DEV = 128
SEQUENCE_LENGTH = 4096
HD = 4096
TOTAL_TOKENS = 4096
COL_BLOCK = 256
N_ROW = 32
N_COL = 16


def draw_log_decay(key, part):
    key = jax.random.fold_in(key, 11)
    variety_random_key, jitter_random_key, spike_random_key, decay_depth_key = jax.random.split(key, 4)
    slow_share = 0.5
    slow_heads = jax.random.uniform(variety_random_key, (LOCAL_HEADS, 1)) < slow_share
    jitter_amount = jnp.exp(jax.random.uniform(jitter_random_key, (LOCAL_HEADS, TOTAL_TOKENS), minval=-0.7, maxval=0.7))
    baseline_rate = jnp.where(slow_heads, 0.5 / SEQUENCE_LENGTH, 1.0 / 40.0)
    spike_events = jax.random.uniform(spike_random_key, (LOCAL_HEADS, TOTAL_TOKENS)) < 2.0 / SEQUENCE_LENGTH
    decay_depth = jnp.log(jax.random.uniform(decay_depth_key, (LOCAL_HEADS, TOTAL_TOKENS), minval=0.5, maxval=0.8))
    return jnp.where(spike_events, decay_depth, -baseline_rate * jitter_amount).astype(jnp.float32)


def strengthened(result, key, source, target, parts, factor):
    owner, partner = [(jnp.arange(result.shape[dim]) // (result.shape[dim] // parts)).reshape([-1 if axis == dim else 1 for axis in range(result.ndim)]) for dim in (source, target)]
    chosen = jax.random.permutation(key, parts)[partner]
    strong = (owner == chosen) | (owner == (partner + parts // 2) % parts)
    return jnp.where(strong, factor * result, result)


def steps_of(stream_key, extent, cuts, least, largest):
    def one(dim, shards_of):
        heights = jax.random.uniform(jax.random.fold_in(jax.random.fold_in(stream_key, 6), dim), (shards_of,), jnp.float32, least / len(cuts), largest / len(cuts))
        return jnp.repeat(jnp.exp(heights), extent[dim] // shards_of).reshape((-1,) + (1,) * (len(extent) - dim - 1))

    gain = one(*cuts[0])
    for cut in cuts[1:]:
        gain = gain * one(*cut)
    return gain


def gaussian(rng, extent, width, bound, cuts=(), held_as=jnp.bfloat16):
    entries = width * jax.random.normal(rng, extent, jnp.float32)
    if cuts:
        entries = entries * steps_of(rng, extent, cuts, -0.22, 0.18)
    return jnp.clip(entries, -bound, bound).astype(held_as)


def noise_with(stream_key, dims, scale, most, cuts, heavy, dtype=jnp.bfloat16):
    entries = scale * jax.random.normal(stream_key, dims, jnp.float32)
    if cuts:
        entries = entries * steps_of(stream_key, dims, cuts, -0.22, 0.18)
    return jnp.clip(strengthened(entries, jax.random.fold_in(stream_key, 3), *heavy), -most, most).astype(dtype)


def setup_inputs(seed: int = 0) -> dict:
    streams_of = jax.random.split(jax.random.key(seed), 9)
    activations = noise_with(streams_of[0], (TOTAL_TOKENS, D), 1.0, 6.0, ((0, 32), (1, 16)), (0, 1, 32, 2.75))
    w_value = noise_with(streams_of[1], (D, HD), D ** -0.5, 0.125, ((0, 32), (1, 16)), (1, 0, 32, 2.75))
    query_input = gaussian(streams_of[2], (TOTAL_TOKENS, HD), 1.0, 6.0, ((0, 32), (1, 16)))
    key_input = gaussian(streams_of[3], (TOTAL_TOKENS, HD), 1.0, 6.0, ((0, 32), (1, 16)))
    log_decay = draw_log_decay(jax.random.fold_in(streams_of[8], 71), 0)
    write_rate = jnp.clip(jnp.exp(math.log(0.2) - 2.3025851 * jax.random.uniform(streams_of[5], (LOCAL_HEADS, TOTAL_TOKENS), jnp.float32) ** steps_of(streams_of[5], (LOCAL_HEADS, TOTAL_TOKENS), ((0, 16), (1, 32)), -0.2, 0.2)), 0.02, 0.2)
    norm_gain = jnp.clip(1.0 + 0.18 * jax.random.normal(streams_of[6], (DH,), jnp.float32), 0.1, 1.9)
    out_grad = gaussian(streams_of[7], (TOTAL_TOKENS, HD), 1.0, 6.0, ((0, 32), (1, 16)))
    return {"activations": activations, "w_value": w_value, "query_input": query_input, "key_input": key_input, "log_decay": log_decay, "write_rate": write_rate, "norm_gain": norm_gain, "out_grad": out_grad}


exact_mode = lax.Precision.HIGHEST

def head_norm(values, norm_gain):
    mean_sq = lax.optimization_barrier(jnp.mean(values * values, axis=-1, keepdims=True))
    return values * lax.rsqrt(mean_sq + 1e-06) * norm_gain

def unit_rows(matrix):
    return matrix * lax.rsqrt(lax.optimization_barrier(jnp.sum(matrix * matrix, axis=-1, keepdims=True)) + 1e-06)

def recurrence(values, queries, key_rows, log_decay, write_rate):
    unit_keys = unit_rows(key_rows)
    decays = jnp.exp(log_decay).T
    rates = write_rate.T
    resets = jnp.arange(TOTAL_TOKENS) % SEQUENCE_LENGTH == 0

    def advance(memory, inputs):
        value_now, query_now, key_now, decay_now, rate_now, reset_now = inputs
        memory = jnp.where(reset_now, jnp.zeros_like(memory), memory)
        faded = decay_now[:, None, None] * memory
        recalled = jnp.einsum('hvk,hk->hv', faded, key_now, precision=exact_mode)
        memory = faded + rate_now[:, None, None] * jnp.einsum('hv,hk->hvk', value_now - recalled, key_now, precision=exact_mode)
        reading = jnp.einsum('hvk,hk->hv', memory, query_now, precision=exact_mode)
        return (memory, reading)
    start_memory = jnp.zeros((LOCAL_HEADS, DH, DH), jnp.float32)
    final_memory, readings = lax.scan(advance, start_memory, (values, queries, unit_keys, decays, rates, resets))
    return readings

def reference(activations, w_value, query_input, key_input, log_decay, write_rate, norm_gain, out_grad):
    value_proj = jnp.dot(activations, w_value, preferred_element_type=jnp.float32).astype(jnp.bfloat16)

    def split_heads(matrix):
        return matrix.astype(jnp.float32).reshape(TOTAL_TOKENS, LOCAL_HEADS, DH)

    def layer_heads(values, queries, key_rows):
        return head_norm(recurrence(values, queries, key_rows, log_decay, write_rate), norm_gain)
    normed, pullback = jax.vjp(layer_heads, split_heads(value_proj), split_heads(query_input), split_heads(key_input))
    value_grad, query_grad, key_grad = pullback(split_heads(out_grad))
    layer_out = normed.reshape(TOTAL_TOKENS, HD).astype(jnp.bfloat16)
    d_value = value_grad.reshape(TOTAL_TOKENS, HD).astype(jnp.bfloat16)
    d_query = query_grad.reshape(TOTAL_TOKENS, HD).astype(jnp.bfloat16)
    d_key = key_grad.reshape(TOTAL_TOKENS, HD).astype(jnp.bfloat16)
    input_sum = jnp.zeros((TOTAL_TOKENS, D), jnp.float32)
    for group_idx in range(N_COL):
        first_col = group_idx * COL_BLOCK
        partial_value = lax.dot_general(d_value[:, first_col:first_col + COL_BLOCK], w_value[:, first_col:first_col + COL_BLOCK], (((1,), (1,)), ((), ())), preferred_element_type=jnp.float32).astype(jnp.bfloat16)
        input_sum = input_sum + lax.optimization_barrier(partial_value).astype(jnp.float32)
    weight_sum = jnp.zeros((D, HD), jnp.float32)
    for group_idx in range(N_ROW):
        first_row = group_idx * TOK_DEV
        partial_value = lax.dot_general(activations[first_row:first_row + TOK_DEV], d_value[first_row:first_row + TOK_DEV], (((0,), (0,)), ((), ())), preferred_element_type=jnp.float32).astype(jnp.bfloat16)
        weight_sum = weight_sum + lax.optimization_barrier(partial_value).astype(jnp.float32)
    return (layer_out, input_sum.astype(jnp.bfloat16), d_query, d_key, weight_sum)
```

```python
import functools

import jax
import jax.numpy as jnp
from jax import lax
from jax.experimental import pallas as pl
from jax.experimental.pallas import tpu as pltpu
from jax.sharding import PartitionSpec as P

MESH = pl.DeviceIdType.MESH
f32 = jnp.float32
bf16 = jnp.bfloat16
NN = (((1,), (0,)), ((), ()))
NT = (((1,), (1,)), ((), ()))
TN = (((0,), (0,)), ((), ()))


def dot(a, b, dims):
    return lax.dot_general(a, b, dims, preferred_element_type=f32)


def halves(a):
    high = a.astype(bf16)
    return high, (a - high.astype(f32)).astype(bf16)


def dot_left(a, b, dims):
    high, low = halves(a)
    return dot(high, b, dims) + dot(low, b, dims)


def dot_both(a, b, dims):
    a_high, a_low = halves(a)
    b_high, b_low = halves(b)
    return dot(a_high, b_high, dims) + (dot(a_high, b_low, dims) + dot(a_low, b_high, dims))


def key_terms(h, q, x, ld, wr, st):
    n = x.shape[0]
    rows = lax.broadcasted_iota(jnp.int32, (n, n), 0)
    cols = lax.broadcasted_iota(jnp.int32, (n, n), 1)
    lower = rows >= cols
    strict = rows > cols
    eye = rows == cols

    def col_of(row):
        return jnp.sum(jnp.where(eye, row, 0.0), axis=1, keepdims=True)

    def row_of(col):
        return jnp.sum(jnp.where(eye, col, 0.0), axis=0, keepdims=True)

    xf = x.astype(f32)
    rs = lax.rsqrt(jnp.sum(xf * xf, axis=1, keepdims=True) + 1e-06)
    rs_row = row_of(rs)
    g = jnp.sum(jnp.where(lower, ld, 0.0), axis=1, keepdims=True)
    g_row = row_of(g)
    total = jnp.sum(ld, axis=1, keepdims=True)
    decay = jnp.exp(g)
    decay_row = jnp.exp(g_row)
    tail = jnp.exp(total - g)
    b = col_of(wr)
    within = jnp.where(lower, jnp.exp(jnp.where(lower, g - g_row, 0.0)), 0.0)
    gram = dot(x, x, NT) * (rs * rs_row)
    coupling = jnp.where(strict, b * within * gram, 0.0)
    ident = jnp.where(eye, 1.0, 0.0)
    near = jnp.where((rows // 16) == (cols // 16), coupling, 0.0)
    inv = ident - near
    power = near
    for _ in range(3):
        power = dot_both(power, power, NN)
        inv = inv + dot_both(inv, power, NN)
    size = 16
    while size < n:
        off = ((rows // (2 * size)) == (cols // (2 * size))) & ((rows // size) != (cols // size))
        part = jnp.where(off, coupling, 0.0)
        inv = inv - dot_both(dot_both(inv, part, NN), inv, NN)
        size *= 2
    carry = dot_left(inv * (wr * decay_row * rs_row), x, NN)
    read = dot(q, x, NT) * within * rs_row
    loss = dot_left(carry * (tail * rs), x, TN) + jnp.where(eye, 1.0 - jnp.exp(total), 0.0)
    st["inv"][h] = inv
    st["within"][h] = within
    st["carry"][h] = carry
    st["read"][h] = read
    lanes = jnp.zeros((n, 128), f32)
    lane = lax.broadcasted_iota(jnp.int32, (n, 128), 1)
    for i, c in enumerate((rs, decay, tail, b)):
        lanes = jnp.where(lane == i, c, lanes)
    st["cols"][h] = lanes
    st["loss"][h] = loss.astype(bf16)


def chain_kernel(
    v_ref, q_ref, x_ref, og_ref, ld_ref, wr_ref, gain_ref,
    out_ref, dq_ref, dk_ref, dv_ref,
    inv, within, carry, read, cols, loss, fresh, grad_raw, summed,
    add, add2, loss_all, got, got2, sent, sent2, state, grad,
    loss_send, loss_recv, s_send, s_recv, b_send, b_recv, t_send, t_recv, u_send, u_recv,
):
    n_row = 32
    me, col = lax.axis_index("row"), lax.axis_index("col")
    head = me // 16
    slot = (me % 16) // 2
    worker = me % 2 == 0
    st = dict(inv=inv, within=within, carry=carry, read=read, cols=cols, loss=loss)

    barrier = pltpu.get_barrier_semaphore()

    def greet(i, _):
        @pl.when(i != me)
        def _():
            pl.semaphore_signal(barrier, inc=1, device_id=(i, col), device_id_type=MESH)
        return 0

    lax.fori_loop(0, n_row, greet, 0)

    for h in range(2):
        part = slice(h * 128, (h + 1) * 128)
        key_terms(h, q_ref[:, part], x_ref[:, part], ld_ref[h : h + 1, :], wr_ref[h : h + 1, :], st)
    pl.semaphore_wait(barrier, n_row - 1)

    def spread(count, to_of, src_of, dst, send_sem, recv_sem):
        def one(i, _):
            to = to_of(i)

            @pl.when(to != me)
            def _():
                pltpu.make_async_remote_copy(
                    src_ref=src_of(i), dst_ref=dst, send_sem=send_sem, recv_sem=recv_sem,
                    device_id=(to, col), device_id_type=MESH,
                ).start()

            @pl.when(to == me)
            def _():
                pltpu.make_async_copy(src_of(i), dst, recv_sem).start()
            return 0

        lax.fori_loop(0, count, one, 0)

    def worker_row(i):
        return (i // 8) * 16 + (i % 8) * 2

    def landed(ref, sem):
        pltpu.make_async_copy(ref, ref, sem).wait()

    spread(16, worker_row, lambda i: loss.at[i // 8], loss_all.at[me], loss_send, loss_recv)

    for h in range(2):
        part = slice(h * 128, (h + 1) * 128)
        c = cols[h]
        rs, tail = c[:, 0:1], c[:, 2:3]
        u = dot_left(inv[h] * wr_ref[h : h + 1, :], v_ref[:, part], NN)
        fresh[h] = u
        add[h] = dot_left(u * (tail * rs), x_ref[:, part], TN).astype(bf16)

    def block(ref):
        return lambda i: ref.at[i // 8, pl.ds(pl.multiple_of((i % 8) * 16, 16), 16), :]

    home = pl.ds(pl.multiple_of(slot * 16, 16), 16)
    spread(16, worker_row, block(add), got.at[me], s_send, s_recv)

    @pl.when(worker)
    def _():
        landed(loss_all, loss_recv)
        landed(got, s_recv)

        def step(i, s):
            s_low = s.astype(bf16)
            sent[i] = s_low
            return s - dot(s_low, loss_all[i], NN) + got[i].astype(f32)

        lax.fori_loop(0, n_row, step, jnp.zeros((16, 128), f32))
        spread(n_row, lambda i: i, lambda i: sent.at[i], state.at[head, home, :], b_send, b_recv)

    landed(state, b_recv)

    gain = gain_ref[0:1, :]
    for h in range(2):
        part = slice(h * 128, (h + 1) * 128)
        c = cols[h]
        decay = c[:, 1:2]
        s = state[h]
        u = fresh[h] - dot_left(carry[h], s, NT)
        fresh[h] = u
        raw = decay * dot(q_ref[:, part], s, NT) + dot_both(read[h], u, NN)
        r = lax.rsqrt(jnp.mean(raw * raw, axis=1, keepdims=True) + 1e-06)
        out_ref[:, part] = (raw * r * gain).astype(bf16)
        gg = og_ref[:, part].astype(f32) * gain
        d_raw = r * gg - raw * (r * r * r * jnp.mean(raw * gg, axis=1, keepdims=True))
        grad_raw[h] = d_raw
        z = dot_both(read[h], d_raw, TN)
        summed[h] = z
        add2[h] = (dot_left(decay * d_raw, q_ref[:, part], TN) - dot_both(z, carry[h], TN)).astype(bf16)

    spread(16, worker_row, block(add2), got2.at[me], t_send, t_recv)

    @pl.when(worker)
    def _():
        landed(got2, t_recv)

        def step(k, s):
            i = n_row - 1 - k
            s_low = s.astype(bf16)
            sent2[i] = s_low
            return s - dot(s_low, loss_all[i], NT) + got2[i].astype(f32)

        lax.fori_loop(0, n_row, step, jnp.zeros((16, 128), f32))
        spread(n_row, lambda i: i, lambda i: sent2.at[i], grad.at[head, home, :], u_send, u_recv)

    landed(grad, u_recv)

    n = 128
    rows_i = lax.broadcasted_iota(jnp.int32, (n, n), 0)
    cols_i = lax.broadcasted_iota(jnp.int32, (n, n), 1)
    for h in range(2):
        part = slice(h * 128, (h + 1) * 128)
        q, x = q_ref[:, part], x_ref[:, part]
        c = cols[h]
        rs, decay, tail, b = c[:, 0:1], c[:, 1:2], c[:, 2:3], c[:, 3:4]
        s, g, u, d_raw = state[h], grad[h], fresh[h], grad_raw[h]
        rs_row = jnp.sum(jnp.where(rows_i == cols_i, rs, 0.0), axis=0, keepdims=True)
        d_u = summed[h] + (tail * rs) * dot(x, g, NT)
        y = dot_both(inv[h], d_u, TN)
        dv_ref[:, part] = (b * y).astype(bf16)
        d_read = dot_both(d_raw, u, NT) * within[h]
        dq_ref[:, part] = (decay * dot_left(d_raw, s, NN) + dot_left(d_read * rs_row, x, NN)).astype(bf16)
        d_gram = jnp.where(rows_i > cols_i, -b * within[h] * dot_both(y, u, NT), 0.0)
        d_k = (
            dot_left(d_read, q, TN)
            + tail * dot_left(u, g, NN)
            - (b * decay) * dot_left(y, s, NN)
            + dot_left(d_gram * rs_row, x, NN)
            + dot_left(d_gram * rs, x, TN)
        )
        unit = rs * x.astype(f32)
        dk_ref[:, part] = (rs * (d_k - unit * jnp.sum(unit * d_k, axis=1, keepdims=True))).astype(bf16)

    def left(ref, sem):
        pltpu.make_async_copy(ref, ref, sem).wait()

    def drain(ref_block, count, sem):
        def one(i, _):
            pltpu.make_async_copy(ref_block, ref_block, sem).wait()
            return 0
        lax.fori_loop(0, count, one, 0)

    own = jnp.where(worker, 1, 0)
    drain(loss.at[0], 16 - own, loss_send)
    drain(got.at[0], 16 - own, s_send)
    drain(got2.at[0], 16 - own, t_send)

    @pl.when(worker)
    def _():
        drain(got.at[0], n_row - 1, b_send)
        drain(got2.at[0], n_row - 1, u_send)


def chain(v, q, x, og, ld, wr, gain):
    sq = (2, 128, 128)
    vm = pl.BlockSpec(memory_space=pltpu.VMEM)
    o = jax.ShapeDtypeStruct((128, 256), bf16)
    dma = pltpu.SemaphoreType.DMA
    return pl.pallas_call(
        chain_kernel,
        out_shape=(o, o, o, o),
        in_specs=[vm] * 7,
        out_specs=(vm,) * 4,
        scratch_shapes=[
            pltpu.VMEM(sq, f32), pltpu.VMEM(sq, f32), pltpu.VMEM(sq, f32), pltpu.VMEM(sq, f32),
            pltpu.VMEM(sq, f32), pltpu.VMEM(sq, bf16), pltpu.VMEM(sq, f32), pltpu.VMEM(sq, f32),
            pltpu.VMEM(sq, f32),
            pltpu.VMEM(sq, bf16), pltpu.VMEM(sq, bf16), pltpu.VMEM((32, 128, 128), bf16),
            pltpu.VMEM((32, 16, 128), bf16), pltpu.VMEM((32, 16, 128), bf16),
            pltpu.VMEM((32, 16, 128), bf16), pltpu.VMEM((32, 16, 128), bf16),
            pltpu.VMEM(sq, bf16), pltpu.VMEM(sq, bf16),
        ] + [dma] * 10,
        compiler_params=pltpu.CompilerParams(
            collective_id=1, has_side_effects=True, vmem_limit_bytes=40 * 1024 * 1024
        ),
        name="chain",
    )(v, q, x, og, ld, wr, gain)


def shards(
    activations, w_value, query_input, key_input, log_decay, write_rate, norm_gain, out_grad
):
    gathered = lax.all_gather(activations, "col", axis=1, tiled=True)
    weight_cols = lax.all_gather(w_value, "row", axis=0, tiled=True)
    value_sum = jnp.dot(gathered, weight_cols, preferred_element_type=jnp.float32)
    value_proj = value_sum.astype(jnp.bfloat16)
    chain_len = lax.axis_size("row")
    layer_out, d_query, d_key, d_value = chain(
        value_proj, query_input, key_input, out_grad, log_decay, write_rate,
        norm_gain.reshape(1, -1),
    )
    partials = lax.dot_general(
        d_value, weight_cols, (((1,), (1,)), ((), ())), preferred_element_type=jnp.float32
    )
    d_input = lax.psum_scatter(
        partials.astype(jnp.bfloat16), "col", scatter_dimension=1, tiled=True
    )
    weight_term = lax.dot_general(
        gathered, d_value, (((0,), (0,)), ((), ())), preferred_element_type=jnp.float32
    ).astype(jnp.bfloat16)
    owned_rows = w_value.shape[0]
    stacked = weight_term.reshape(chain_len, owned_rows, weight_term.shape[1])
    received = lax.all_to_all(stacked, "row", split_axis=0, concat_axis=0, tiled=True)
    d_w_value = jnp.sum(received.astype(jnp.float32), axis=0)
    return (layer_out, d_input, d_query, d_key, d_w_value)


def solution(mesh):
    in_specs = (
        P("row", "col"),
        P("row", "col"),
        P("row", "col"),
        P("row", "col"),
        P("col", "row"),
        P("col", "row"),
        P(),
        P("row", "col"),
    )
    out_specs = (
        P("row", "col"),
        P("row", "col"),
        P("row", "col"),
        P("row", "col"),
        P("row", "col"),
    )
    return jax.shard_map(shards, mesh=mesh, in_specs=in_specs, out_specs=out_specs, check_vma=False)
```

```python
import functools

import jax
import jax.numpy as jnp
from jax import lax
from jax.experimental import pallas as pl
from jax.experimental.pallas import tpu as pltpu
from jax.sharding import PartitionSpec as P

MESH = pl.DeviceIdType.MESH
f32 = jnp.float32
bf16 = jnp.bfloat16
NN = (((1,), (0,)), ((), ()))
NT = (((1,), (1,)), ((), ()))
TN = (((0,), (0,)), ((), ()))


def dot(a, b, dims):
    return lax.dot_general(a, b, dims, preferred_element_type=f32)


def halves(a):
    high = a.astype(bf16)
    return high, (a - high.astype(f32)).astype(bf16)


def dot_left(a, b, dims):
    high, low = halves(a)
    return dot(high, b, dims) + dot(low, b, dims)


def dot_both(a, b, dims):
    a_high, a_low = halves(a)
    b_high, b_low = halves(b)
    return dot(a_high, b_high, dims) + (dot(a_high, b_low, dims) + dot(a_low, b_high, dims))


def key_terms(h, q, x, ld, wr, st):
    n = x.shape[0]
    rows = lax.broadcasted_iota(jnp.int32, (n, n), 0)
    cols = lax.broadcasted_iota(jnp.int32, (n, n), 1)
    lower = rows >= cols
    strict = rows > cols
    eye = rows == cols

    def col_of(row):
        return jnp.sum(jnp.where(eye, row, 0.0), axis=1, keepdims=True)

    def row_of(col):
        return jnp.sum(jnp.where(eye, col, 0.0), axis=0, keepdims=True)

    xf = x.astype(f32)
    rs = lax.rsqrt(jnp.sum(xf * xf, axis=1, keepdims=True) + 1e-06)
    rs_row = row_of(rs)
    g = jnp.sum(jnp.where(lower, ld, 0.0), axis=1, keepdims=True)
    g_row = row_of(g)
    total = jnp.sum(ld, axis=1, keepdims=True)
    decay = jnp.exp(g)
    decay_row = jnp.exp(g_row)
    tail = jnp.exp(total - g)
    b = col_of(wr)
    within = jnp.where(lower, jnp.exp(jnp.where(lower, g - g_row, 0.0)), 0.0)
    gram = dot(x, x, NT) * (rs * rs_row)
    coupling = jnp.where(strict, b * within * gram, 0.0)
    ident = jnp.where(eye, 1.0, 0.0)
    near = jnp.where((rows // 16) == (cols // 16), coupling, 0.0)
    inv = ident - near
    power = near
    yield
    for _ in range(3):
        power = dot_both(power, power, NN)
        inv = inv + dot_both(inv, power, NN)
        yield
    size = 16
    while size < n:
        off = ((rows // (2 * size)) == (cols // (2 * size))) & ((rows // size) != (cols // size))
        part = jnp.where(off, coupling, 0.0)
        inv = inv - dot_both(dot_both(inv, part, NN), inv, NN)
        size *= 2
        yield
    st["inv"][h] = inv
    st["within"][h] = within
    carry = dot_left(inv * (wr * decay_row * rs_row), x, NN)
    read = dot(q, x, NT) * within * rs_row
    loss = dot_left(carry * (tail * rs), x, TN) + jnp.where(eye, 1.0 - jnp.exp(total), 0.0)
    st["carry"][h] = carry
    st["read"][h] = read
    lanes = jnp.zeros((n, 128), f32)
    lane = lax.broadcasted_iota(jnp.int32, (n, 128), 1)
    for i, c in enumerate((rs, decay, tail, b)):
        lanes = jnp.where(lane == i, c, lanes)
    st["cols"][h] = lanes
    st["loss"][h] = loss.astype(bf16)


def layer_kernel(
    act_ref, w_ref, q_ref, x_ref, og_ref, ld_ref, wr_ref, gain_ref,
    out_ref, din_ref, dq_ref, dk_ref, dw_ref,
    inv, within, carry, read, cols, loss, fresh, grad_raw, summed, v_ref,
    act_own, act_all, w_all, part, part_in, loss_all,
    add, add2, got, got2, sent, sent2, state, grad,
    dv_all, w_terms, w_right, w_left, in_terms, in_sib, in_near, in_far, in_last,
    act_sem, act_sent, w_sem, w_sent, part_sem, loss_sem, loss_sent,
    s_send, s_recv, b_send, b_recv, t_send, t_recv, u_send, u_recv,
    dv_sem, r_sem, r_sent, i_sent, sib_sem, near_sem, far_sem, last_sem,
):
    n_row, n_z = 32, 16
    me, col = lax.axis_index("row"), lax.axis_index("col")
    a, z = me // n_z, me % n_z
    other = (1 - a) * n_z + z
    y, x_hi, core = col // 4, (col // 2) % 2, col % 2
    twin = col + 1 - 2 * core
    y_near = y + 1 - 2 * (y % 2)
    col_near = y_near * 4 + x_hi * 2 + core
    col_far = (3 - y) * 4 + x_hi * 2 + core
    source = a == y // 2
    first = jnp.where(source, y % 2, 1 - y % 2)
    slot = z // 2
    worker = z % 2 == 0
    up, down = a * n_z + (z + 1) % n_z, a * n_z + (z + n_z - 1) % n_z

    barrier = pltpu.get_barrier_semaphore()

    def greet(i, _):
        @pl.when(i != me)
        def _():
            pl.semaphore_signal(barrier, inc=1, device_id=(i, col), device_id_type=MESH)
        return 0

    lax.fori_loop(0, n_row, greet, 0)
    col_side = y * 4 + (1 - x_hi) * 2 + core
    for row_to, col_to in (
        (me, twin), (me, col_near), (me, col_far), (me, col_side), (other, col_side)
    ):
        pl.semaphore_signal(barrier, inc=1, device_id=(row_to, col_to), device_id_type=MESH)
    for i in range(2):
        act_own[i] = act_ref[:, i * 256 : (i + 1) * 256]
    pl.semaphore_wait(barrier, n_row - 1 + 5)

    def remote(src, dst, send_sem, recv_sem, row_to, col_to):
        pltpu.make_async_remote_copy(
            src_ref=src, dst_ref=dst, send_sem=send_sem, recv_sem=recv_sem,
            device_id=(row_to, col_to), device_id_type=MESH,
        ).start()

    def landed(ref, sem):
        pltpu.make_async_copy(ref, ref, sem).wait()

    home_row = (y // 2) * n_z + z
    for xh in range(2):
        to_col = y * 4 + xh * 2 + core
        here = source & (x_hi == xh)
        dst = act_all.at[a, col % 8]

        @pl.when(jnp.logical_not(here))
        def _():
            remote(act_own, dst, act_sent, act_sem.at[a, col % 8], home_row, to_col)

        @pl.when(here)
        def _():
            pltpu.make_async_copy(act_own, dst, act_sem.at[a, col % 8]).start()

    def act_first(i):
        t, xh = i // 2, i % 2
        cc = first * 4 + xh * 2 + core
        ref, sem = act_all.at[t, cc], act_sem.at[t, cc]
        landed(ref, sem)

        @pl.when(source)
        def _():
            remote(ref, ref, act_sent, sem, me, col_far)

        remote(ref, ref, act_sent, sem, me, col_near)
        remote(ref, ref, act_sent, sem, me, twin)

    def act_second(i):
        t, xh = i // 2, i % 2
        cc = (1 - first) * 4 + xh * 2 + core
        ref, sem = act_all.at[t, cc], act_sem.at[t, cc]
        landed(ref, sem)
        remote(ref, ref, act_sent, sem, me, twin)

    def act_last():
        for t in range(2):
            for k in range(4):
                cc = k * 2 + (1 - core)
                landed(act_all.at[t, cc], act_sem.at[t, cc])

    w_all[z] = w_ref[...]

    def w_piece(s, way, sub, origin):
        ref = w_all.at[origin, pl.ds(sub * 128, 128), :]
        return ref, w_sem.at[way, s, sub]

    def w_send(s, way):
        origin = (z + n_z - s) % n_z if way == 0 else (z + s) % n_z
        for sub in range(2):
            ref, sem = w_piece(s, way, sub, origin)
            remote(ref, ref, w_sent, sem, up if way == 0 else down, col)

    def w_step(s):
        for sub in range(2):
            for way in range(2):
                if way == 1 and s == 7:
                    continue
                origin = (z + n_z - s - 1) % n_z if way == 0 else (z + s + 1) % n_z
                ref, sem = w_piece(s, way, sub, origin)
                landed(ref, sem)
                if s + 1 < (8 if way == 0 else 7):
                    _, after = w_piece(s + 1, way, sub, origin)
                    remote(ref, ref, w_sent, after, up if way == 0 else down, col)

    w_send(0, 0)
    w_send(0, 1)

    def loss_start():
        loss_all[z, a] = loss[a]
        remote(loss.at[1 - a], loss_all.at[z, a], loss_sent.at[0], loss_sem.at[2, 0], other, col)

    def loss_first():
        landed(loss_all.at[z, 1 - a], loss_sem.at[2, 0])
        for way in range(2):
            remote(loss_all.at[z], loss_all.at[z], loss_sent.at[1], loss_sem.at[way, 0],
                   up if way == 0 else down, col)

    def loss_step(s):
        for way in range(2):
            if way == 1 and s == 7:
                continue
            origin = (z + n_z - s - 1) % n_z if way == 0 else (z + s + 1) % n_z
            landed(loss_all.at[origin], loss_sem.at[way, s])
            if s + 1 < (8 if way == 0 else 7):
                remote(loss_all.at[origin], loss_all.at[origin], loss_sent.at[1],
                       loss_sem.at[way, s + 1], up if way == 0 else down, col)

    st = dict(inv=inv, within=within, carry=carry, read=read, cols=cols, loss=loss)
    local = []
    for h in range(2):
        p = slice(h * 128, (h + 1) * 128)
        local.append(
            key_terms(h, q_ref[:, p], x_ref[:, p], ld_ref[h : h + 1, :], wr_ref[h : h + 1, :], st)
        )

    def think():
        for terms in local:
            next(terms, None)

    think()
    think()
    w_step(0)
    think()
    think()
    act_first(0)
    act_first(1)
    w_step(1)
    think()
    act_first(2)
    act_first(3)
    w_step(2)
    think()
    w_step(3)
    think()
    think()
    loss_start()
    w_step(4)
    act_second(0)
    act_second(1)
    loss_first()
    w_step(5)
    act_second(2)
    act_second(3)
    loss_step(0)
    w_step(6)
    loss_step(1)
    w_step(7)
    loss_step(2)
    act_last()
    loss_step(3)

    total = jnp.zeros((256, 256), f32)
    for k in range(n_z):
        both = jnp.concatenate([act_all[0, k // 2, k % 2], act_all[1, k // 2, k % 2]], axis=0)
        total = total + dot(both, w_all[k], NN)
    part[0] = total[:128]
    part[1] = total[128:]
    remote(part.at[1 - a], part_in, part_sem.at[0], part_sem.at[1], other, col)
    loss_step(4)
    landed(part_in, part_sem.at[1])
    v_ref[...] = (part[a] + part_in[...]).astype(bf16)
    loss_step(5)

    def spread(count, to_of, src_of, dst, send_sem, recv_sem):
        def one(i, _):
            to = to_of(i)

            @pl.when(to != me)
            def _():
                remote(src_of(i), dst, send_sem, recv_sem, to, col)

            @pl.when(to == me)
            def _():
                pltpu.make_async_copy(src_of(i), dst, recv_sem).start()
            return 0

        lax.fori_loop(0, count, one, 0)

    def worker_row(i):
        return (i // 8) * 16 + (i % 8) * 2

    for h in range(2):
        p = slice(h * 128, (h + 1) * 128)
        c = cols[h]
        rs, tail = c[:, 0:1], c[:, 2:3]
        u = dot_left(inv[h] * wr_ref[h : h + 1, :], v_ref[:, p], NN)
        fresh[h] = u
        add[h] = dot_left(u * (tail * rs), x_ref[:, p], TN).astype(bf16)

    def block(ref):
        return lambda i: ref.at[i // 8, pl.ds(pl.multiple_of((i % 8) * 16, 16), 16), :]

    home = pl.ds(pl.multiple_of(slot * 16, 16), 16)
    spread(16, worker_row, block(add), got.at[me], s_send, s_recv)
    loss_step(6)
    loss_step(7)

    @pl.when(worker)
    def _():
        landed(got, s_recv)

        def step(i, s):
            s_low = s.astype(bf16)
            sent[i] = s_low
            return s - dot(s_low, loss_all[i % 16, i // 16], NN) + got[i].astype(f32)

        lax.fori_loop(0, n_row, step, jnp.zeros((16, 128), f32))
        spread(n_row, lambda i: i, lambda i: sent.at[i], state.at[a, home, :], b_send, b_recv)

    landed(state, b_recv)

    gain = gain_ref[0:1, :]
    for h in range(2):
        p = slice(h * 128, (h + 1) * 128)
        c = cols[h]
        decay = c[:, 1:2]
        s = state[h]
        u = fresh[h] - dot_left(carry[h], s, NT)
        fresh[h] = u
        raw = decay * dot(q_ref[:, p], s, NT) + dot_both(read[h], u, NN)
        r = lax.rsqrt(jnp.mean(raw * raw, axis=1, keepdims=True) + 1e-06)
        out_ref[:, p] = (raw * r * gain).astype(bf16)
        gg = og_ref[:, p].astype(f32) * gain
        d_raw = r * gg - raw * (r * r * r * jnp.mean(raw * gg, axis=1, keepdims=True))
        grad_raw[h] = d_raw
        back = dot_both(read[h], d_raw, TN)
        summed[h] = back
        add2[h] = (dot_left(decay * d_raw, q_ref[:, p], TN) - dot_both(back, carry[h], TN)).astype(bf16)

    spread(16, worker_row, block(add2), got2.at[me], t_send, t_recv)

    @pl.when(worker)
    def _():
        landed(got2, t_recv)

        def step(k, s):
            i = n_row - 1 - k
            s_low = s.astype(bf16)
            sent2[i] = s_low
            return s - dot(s_low, loss_all[i % 16, i // 16], NT) + got2[i].astype(f32)

        lax.fori_loop(0, n_row, step, jnp.zeros((16, 128), f32))
        spread(n_row, lambda i: i, lambda i: sent2.at[i], grad.at[a, home, :], u_send, u_recv)

    landed(grad, u_recv)

    n = 128
    rows_i = lax.broadcasted_iota(jnp.int32, (n, n), 0)
    cols_i = lax.broadcasted_iota(jnp.int32, (n, n), 1)
    own_tokens = pl.ds(pl.multiple_of(a * 128, 128), 128)
    later = []
    for h in range(2):
        p = slice(h * 128, (h + 1) * 128)
        c = cols[h]
        rs, tail, b = c[:, 0:1], c[:, 2:3], c[:, 3:4]
        d_u = summed[h] + (tail * rs) * dot(x_ref[:, p], grad[h], NT)
        grown = dot_both(inv[h], d_u, TN)
        later.append(grown)
        dv_all[own_tokens, p] = (b * grown).astype(bf16)
    mine = dv_all.at[own_tokens, :]
    remote(mine, mine, dv_sem.at[0], dv_sem.at[1], other, col)

    def query_key_grads(h):
        p = slice(h * 128, (h + 1) * 128)
        q, x = q_ref[:, p], x_ref[:, p]
        c = cols[h]
        rs, decay, tail, b = c[:, 0:1], c[:, 1:2], c[:, 2:3], c[:, 3:4]
        s, g, u, d_raw, grown = state[h], grad[h], fresh[h], grad_raw[h], later[h]
        rs_row = jnp.sum(jnp.where(rows_i == cols_i, rs, 0.0), axis=0, keepdims=True)
        d_read = dot_both(d_raw, u, NT) * within[h]
        dq_ref[:, p] = (decay * dot_left(d_raw, s, NN) + dot_left(d_read * rs_row, x, NN)).astype(bf16)
        d_gram = jnp.where(rows_i > cols_i, -b * within[h] * dot_both(grown, u, NT), 0.0)
        d_k = (
            dot_left(d_read, q, TN)
            + tail * dot_left(u, g, NN)
            - (b * decay) * dot_left(grown, s, NN)
            + dot_left(d_gram * rs_row, x, NN)
            + dot_left(d_gram * rs, x, TN)
        )
        unit = rs * x.astype(f32)
        dk_ref[:, p] = (rs * (d_k - unit * jnp.sum(unit * d_k, axis=1, keepdims=True))).astype(bf16)

    theirs = dv_all.at[pl.ds(pl.multiple_of((1 - a) * 128, 128), 128), :]
    landed(theirs, dv_sem.at[1])

    def w_term(d):
        acc = dot(act_all[0, d // 2, d % 2], dv_all[0:128, :], TN)
        return acc + dot(act_all[1, d // 2, d % 2], dv_all[128:256, :], TN)

    def r_dest(s, way):
        return (z + 8 - s) % n_z if way == 0 else (z + n_z - 7 + s) % n_z

    def r_slot(s, way):
        return w_right.at[s] if way == 0 else w_left.at[s]

    def r_send(s, way):
        d = r_dest(s, way)
        for sub in range(2):
            q = pl.ds(sub * 128, 128)
            if s > 0:
                landed(r_slot(s - 1, way).at[q, :], r_sem.at[way, s - 1, sub])
                w_terms[d, q, :] = (
                    w_terms[d, q, :].astype(f32) + r_slot(s - 1, way)[q, :].astype(f32)
                ).astype(bf16)
            remote(w_terms.at[d, q, :], r_slot(s, way).at[q, :], r_sent, r_sem.at[way, s, sub],
                   up if way == 0 else down, col)

    def r_make(s):
        for way in range(2):
            if way == 1 and s == 7:
                continue
            d = r_dest(s, way)
            w_terms[d] = w_term(d).astype(bf16)

    def r_step(s):
        for way in range(2):
            if way == 1 and s == 7:
                continue
            r_send(s, way)

    def in_make(cc):
        for i in range(2):
            both = dot(dv_all[...], w_all[cc * 2 + i], NT).astype(bf16)
            for t in range(2):
                in_terms[t, cc, i] = both[t * 128 : (t + 1) * 128]

    def plus(t, cc, ref):
        in_terms[t, cc] = (in_terms[t, cc].astype(f32) + ref[...].astype(f32)).astype(bf16)

    def sib_send(k):
        cc = k * 2 + 1 - core
        in_make(cc)
        for t in range(2):
            remote(in_terms.at[t, cc], in_sib.at[t, k], i_sent, sib_sem.at[t, k], me, twin)

    def own_make(k):
        in_make(k * 2 + core)

    def near_send(i):
        t, xh = i // 2, i % 2
        k = (1 - first) * 2 + xh
        cc = k * 2 + core
        landed(in_sib.at[t, k], sib_sem.at[t, k])
        plus(t, cc, in_sib.at[t, k])
        remote(in_terms.at[t, cc], in_near.at[t, xh], i_sent, near_sem.at[t, xh], me, col_near)

    def far_send(i):
        t, xh = i // 2, i % 2
        k = first * 2 + xh
        cc = k * 2 + core
        landed(in_sib.at[t, k], sib_sem.at[t, k])
        plus(t, cc, in_sib.at[t, k])
        landed(in_near.at[t, xh], near_sem.at[t, xh])
        plus(t, cc, in_near.at[t, xh])

        @pl.when(jnp.logical_not(source))
        def _():
            remote(in_terms.at[t, cc], in_far.at[t, xh], i_sent, far_sem.at[t, xh], me, col_far)

    def home_send(i):
        t, xh = i // 2, i % 2
        k = first * 2 + xh
        cc = k * 2 + core

        @pl.when(source)
        def _():
            landed(in_far.at[t, xh], far_sem.at[t, xh])
            plus(t, cc, in_far.at[t, xh])
            row_to, col_to = t * n_z + z, y * 4 + xh * 2 + core
            here = (row_to == me) & (col_to == col)

            @pl.when(jnp.logical_not(here))
            def _():
                remote(in_terms.at[t, cc], in_last.at[x_hi], i_sent, last_sem.at[x_hi], row_to, col_to)

            @pl.when(here)
            def _():
                pltpu.make_async_copy(in_terms.at[t, cc], in_last.at[x_hi], last_sem.at[x_hi]).start()

    r_make(0)
    r_step(0)
    for k in range(4):
        sib_send(k)
    r_make(1)
    for k in range(4):
        own_make(k)
    r_step(1)
    r_make(2)
    near_send(0)
    near_send(1)
    near_send(2)
    near_send(3)
    r_step(2)
    r_make(3)
    query_key_grads(0)
    r_step(3)
    r_make(4)
    far_send(0)
    far_send(1)
    r_step(4)
    r_make(5)
    far_send(2)
    far_send(3)
    query_key_grads(1)
    r_step(5)
    r_make(6)
    home_send(0)
    home_send(1)
    r_step(6)
    r_make(7)
    home_send(2)
    home_send(3)
    r_step(7)
    own_term = w_term(z)
    for xh in range(2):
        landed(in_last.at[xh], last_sem.at[xh])
    for i in range(2):
        din_ref[:, i * 256 : (i + 1) * 256] = (
            in_last[0, i].astype(f32) + in_last[1, i].astype(f32)
        ).astype(bf16)
    for sub in range(2):
        q = pl.ds(sub * 128, 128)
        landed(w_right.at[7, q, :], r_sem.at[0, 7, sub])
        landed(w_left.at[6, q, :], r_sem.at[1, 6, sub])
    dw_ref[...] = own_term + w_right[7].astype(f32) + w_left[6].astype(f32)

    def drain(ref, count, sem):
        def one(i, _):
            pltpu.make_async_copy(ref, ref, sem).wait()
            return 0
        lax.fori_loop(0, count, one, 0)

    big = act_own
    own = jnp.where(worker, 1, 0)
    far = jnp.where(source, 1, 0)
    self_home = jnp.where(source, 1, 0)
    drain(big, 2 - self_home + 4 + 4 * far + 8, act_sent)
    drain(w_all.at[0, pl.ds(0, 128), :], 30, w_sent)
    landed(part.at[0], part_sem.at[0])
    landed(loss.at[0], loss_sent.at[0])
    drain(loss_all.at[0], 15, loss_sent.at[1])
    drain(got.at[0], 16 - own, s_send)
    drain(got.at[0], 16 - own, t_send)

    @pl.when(worker)
    def _():
        drain(got.at[0], n_row - 1, b_send)
        drain(got.at[0], n_row - 1, u_send)

    landed(mine, dv_sem.at[0])
    drain(w_all.at[0, pl.ds(0, 128), :], 30, r_sent)
    drain(big, 8 + 4 + 4 * (1 - far) + (4 - 1) * far, i_sent)


def layer(act, w, q, x, og, ld, wr, gain):
    sq = (2, 128, 128)
    vm = pl.BlockSpec(memory_space=pltpu.VMEM)
    o = jax.ShapeDtypeStruct((128, 256), bf16)
    dma = pltpu.SemaphoreType.DMA
    V = pltpu.VMEM
    return pl.pallas_call(
        layer_kernel,
        out_shape=(
            o,
            jax.ShapeDtypeStruct((128, 512), bf16),
            o,
            o,
            jax.ShapeDtypeStruct((256, 256), f32),
        ),
        in_specs=[vm] * 8,
        out_specs=(vm,) * 5,
        scratch_shapes=[
            V(sq, f32), V(sq, f32), V(sq, f32), V(sq, f32), V(sq, f32), V(sq, bf16),
            V(sq, f32), V(sq, f32), V(sq, f32), V((128, 256), bf16),
            V((2, 128, 256), bf16), V((2, 8, 2, 128, 256), bf16), V((16, 256, 256), bf16),
            V((2, 128, 256), f32), V((128, 256), f32), V((16, 2, 128, 128), bf16),
            V(sq, bf16), V(sq, bf16), V((32, 16, 128), bf16), V((32, 16, 128), bf16),
            V((32, 16, 128), bf16), V((32, 16, 128), bf16), V(sq, bf16), V(sq, bf16),
            V((256, 256), bf16), V((16, 256, 256), bf16), V((8, 256, 256), bf16),
            V((7, 256, 256), bf16), V((2, 8, 2, 128, 256), bf16), V((2, 4, 2, 128, 256), bf16),
            V((2, 2, 2, 128, 256), bf16), V((2, 2, 2, 128, 256), bf16), V((2, 2, 128, 256), bf16),
            dma((2, 8)), dma, dma((2, 8, 2)), dma, dma((2,)), dma((3, 8)), dma((2,)),
            dma, dma, dma, dma, dma, dma, dma, dma,
            dma((2,)), dma((2, 8, 2)), dma, dma, dma((2, 4)), dma((2, 2)), dma((2, 2)), dma((2,)),
        ],
        compiler_params=pltpu.CompilerParams(
            collective_id=1, has_side_effects=True, vmem_limit_bytes=48 * 1024 * 1024
        ),
        name="layer",
    )(act, w, q, x, og, ld, wr, gain)


def shards(
    activations, w_value, query_input, key_input, log_decay, write_rate, norm_gain, out_grad
):
    return layer(
        activations, w_value, query_input, key_input, out_grad, log_decay, write_rate,
        norm_gain.reshape(1, -1),
    )


def solution(mesh):
    split = P("row", "col")
    flipped = P("col", "row")
    return jax.shard_map(
        shards,
        mesh=mesh,
        in_specs=(split, split, split, split, flipped, flipped, P(), split),
        out_specs=(split,) * 5,
        check_vma=False,
    )
```

```python
import functools

import jax
import jax.numpy as jnp
from jax import lax
from jax.experimental import pallas as pl
from jax.experimental.pallas import tpu as pltpu
from jax.sharding import PartitionSpec as P

MESH = pl.DeviceIdType.MESH
f32 = jnp.float32
bf16 = jnp.bfloat16
NN = (((1,), (0,)), ((), ()))
NT = (((1,), (1,)), ((), ()))
TN = (((0,), (0,)), ((), ()))


def dot(a, b, dims):
    return lax.dot_general(a, b, dims, preferred_element_type=f32)


def halves(a):
    high = a.astype(bf16)
    return high, (a - high.astype(f32)).astype(bf16)


def dot_left(a, b, dims):
    high, low = halves(a)
    return dot(high, b, dims) + dot(low, b, dims)


def dot_both(a, b, dims):
    a_high, a_low = halves(a)
    b_high, b_low = halves(b)
    return dot(a_high, b_high, dims) + (dot(a_high, b_low, dims) + dot(a_low, b_high, dims))


def key_terms(h, q, x, ld, wr, st):
    n = x.shape[0]
    rows = lax.broadcasted_iota(jnp.int32, (n, n), 0)
    cols = lax.broadcasted_iota(jnp.int32, (n, n), 1)
    lower = rows >= cols
    strict = rows > cols
    eye = rows == cols

    def col_of(row):
        return jnp.sum(jnp.where(eye, row, 0.0), axis=1, keepdims=True)

    def row_of(col):
        return jnp.sum(jnp.where(eye, col, 0.0), axis=0, keepdims=True)

    xf = x.astype(f32)
    rs = lax.rsqrt(jnp.sum(xf * xf, axis=1, keepdims=True) + 1e-06)
    rs_row = row_of(rs)
    g = jnp.sum(jnp.where(lower, ld, 0.0), axis=1, keepdims=True)
    g_row = row_of(g)
    total = jnp.sum(ld, axis=1, keepdims=True)
    decay = jnp.exp(g)
    decay_row = jnp.exp(g_row)
    tail = jnp.exp(total - g)
    b = col_of(wr)
    within = jnp.where(lower, jnp.exp(jnp.where(lower, g - g_row, 0.0)), 0.0)
    gram = dot(x, x, NT) * (rs * rs_row)
    coupling = jnp.where(strict, b * within * gram, 0.0)
    ident = jnp.where(eye, 1.0, 0.0)
    near = jnp.where((rows // 16) == (cols // 16), coupling, 0.0)
    inv = ident - near
    power = near
    yield
    for _ in range(3):
        power = dot_both(power, power, NN)
        inv = inv + dot_both(inv, power, NN)
        yield
    size = 16
    while size < n:
        off = ((rows // (2 * size)) == (cols // (2 * size))) & ((rows // size) != (cols // size))
        part = jnp.where(off, coupling, 0.0)
        inv = inv - dot_both(dot_both(inv, part, NN), inv, NN)
        size *= 2
        yield
    st["inv"][h] = inv
    st["within"][h] = within
    carry = dot_left(inv * (wr * decay_row * rs_row), x, NN)
    read = dot(q, x, NT) * within * rs_row
    loss = dot_left(carry * (tail * rs), x, TN) + jnp.where(eye, 1.0 - jnp.exp(total), 0.0)
    st["carry"][h] = carry
    st["read"][h] = read
    lanes = jnp.zeros((n, 128), f32)
    lane = lax.broadcasted_iota(jnp.int32, (n, 128), 1)
    for i, c in enumerate((rs, decay, tail, b)):
        lanes = jnp.where(lane == i, c, lanes)
    st["cols"][h] = lanes
    st["loss"][h] = loss.astype(bf16)


SUBS = 4
UNROLL = 4
SUB = 256 // SUBS


def layer_kernel(
    act_hbm, w_hbm, q_hbm, x_hbm, og_hbm, ld_hbm, wr_hbm, gain_hbm,
    out_ref, din_ref, dq_ref, dk_ref, dw_ref,
    inv, within, carry, read, cols, loss, fresh, grad_raw, summed, v_ref,
    act_own, act_all, w_all, part, part_in, loss_all,
    add, add2, got, got2, sent, sent2, state, grad,
    dv_all, w_terms, w_right, w_left, in_terms, in_sib, in_near, in_far, in_last,
    act_sem, act_sent, w_sem, w_sent, part_sem, loss_sem, loss_sent,
    s_send, s_recv, b_send, b_recv, t_send, t_recv, u_send, u_recv,
    dv_sem, r_sem, r_sent, i_sent, sib_sem, near_sem, far_sem, last_sem,
    q_ref, x_ref, og_ref, ld_ref, wr_ref, gain_ref, load_sem,
):
    n_row, n_z = 32, 16
    me, col = lax.axis_index("row"), lax.axis_index("col")
    a, z = me // n_z, me % n_z
    other = (1 - a) * n_z + z
    y, x_hi, core = col // 4, (col // 2) % 2, col % 2
    twin = col + 1 - 2 * core
    y_near = y + 1 - 2 * (y % 2)
    col_near = y_near * 4 + x_hi * 2 + core
    col_far = (3 - y) * 4 + x_hi * 2 + core
    source = a == y // 2
    first = jnp.where(source, y % 2, 1 - y % 2)
    slot = z // 2
    worker = z % 2 == 0
    up, down = a * n_z + (z + 1) % n_z, a * n_z + (z + n_z - 1) % n_z

    barrier = pltpu.get_barrier_semaphore()

    col_side = y * 4 + (1 - x_hi) * 2 + core
    for row_to, col_to in (
        (up, col), (down, col), (other, col), (me, twin), (me, col_near), (me, col_far),
        (me, col_side), (other, col_side),
    ):
        pl.semaphore_signal(barrier, inc=1, device_id=(row_to, col_to), device_id_type=MESH)
    w_own = w_all.at[z]
    loads = [
        pltpu.make_async_copy(act_hbm.at[:, pl.ds(i * 256, 256)], act_own.at[i], load_sem.at[i])
        for i in range(2)
    ] + [pltpu.make_async_copy(w_hbm, w_own, load_sem.at[2])]
    more = [
        pltpu.make_async_copy(src, dst, load_sem.at[3 + i])
        for i, (src, dst) in enumerate((
            (q_hbm, q_ref), (x_hbm, x_ref), (og_hbm, og_ref), (ld_hbm, ld_ref), (wr_hbm, wr_ref),
            (gain_hbm, gain_ref),
        ))
    ]
    for load in loads + more:
        load.start()
    for load in loads:
        load.wait()
    pl.semaphore_wait(barrier, 8)

    def remote(src, dst, send_sem, recv_sem, row_to, col_to):
        pltpu.make_async_remote_copy(
            src_ref=src, dst_ref=dst, send_sem=send_sem, recv_sem=recv_sem,
            device_id=(row_to, col_to), device_id_type=MESH,
        ).start()

    def landed(ref, sem):
        pltpu.make_async_copy(ref, ref, sem).wait()

    home_row = (y // 2) * n_z + z
    for xh in range(2):
        to_col = y * 4 + xh * 2 + core
        here = source & (x_hi == xh)
        for f in range(2):
            dst, sem = act_all.at[a, col % 8, f], act_sem.at[a, col % 8, f]

            @pl.when(jnp.logical_not(here))
            def _():
                remote(act_own.at[f], dst, act_sent, sem, home_row, to_col)

            @pl.when(here)
            def _():
                pltpu.make_async_copy(act_own.at[f], dst, sem).start()

    def act_first(i):
        t, xh, f = i // 4, (i // 2) % 2, i % 2
        cc = first * 4 + xh * 2 + core
        ref, sem = act_all.at[t, cc, f], act_sem.at[t, cc, f]
        landed(ref, sem)

        @pl.when(source)
        def _():
            remote(ref, ref, act_sent, sem, me, col_far)

        remote(ref, ref, act_sent, sem, me, col_near)
        remote(ref, ref, act_sent, sem, me, twin)

    def act_second(i):
        t, xh, f = i // 4, (i // 2) % 2, i % 2
        cc = (1 - first) * 4 + xh * 2 + core
        ref, sem = act_all.at[t, cc, f], act_sem.at[t, cc, f]
        landed(ref, sem)
        remote(ref, ref, act_sent, sem, me, twin)

    def act_last():
        for t in range(2):
            for k in range(4):
                cc = k * 2 + (1 - core)
                for f in range(2):
                    landed(act_all.at[t, cc, f], act_sem.at[t, cc, f])

    def w_piece(s, way, sub, origin):
        ref = w_all.at[origin, pl.ds(sub * SUB, SUB), :]
        return ref, w_sem.at[way, s, sub]

    def w_send(s, way):
        origin = (z + n_z - s) % n_z if way == 0 else (z + s) % n_z
        for sub in range(SUBS):
            ref, sem = w_piece(s, way, sub, origin)
            remote(ref, ref, w_sent, sem, up if way == 0 else down, col)

    def w_step(s):
        for sub in range(SUBS):
            for way in range(2):
                if way == 1 and s == 7:
                    continue
                origin = (z + n_z - s - 1) % n_z if way == 0 else (z + s + 1) % n_z
                ref, sem = w_piece(s, way, sub, origin)
                landed(ref, sem)
                if s + 1 < (8 if way == 0 else 7):
                    _, after = w_piece(s + 1, way, sub, origin)
                    remote(ref, ref, w_sent, after, up if way == 0 else down, col)

    w_send(0, 0)
    w_send(0, 1)

    def loss_start():
        loss_all[z, a] = loss[a]
        remote(loss.at[1 - a], loss_all.at[z, a], loss_sent.at[0], loss_sem.at[2, 0], other, col)

    def loss_first():
        landed(loss_all.at[z, 1 - a], loss_sem.at[2, 0])
        for way in range(2):
            remote(loss_all.at[z], loss_all.at[z], loss_sent.at[1], loss_sem.at[way, 0],
                   up if way == 0 else down, col)

    def loss_step(s):
        for way in range(2):
            if way == 1 and s == 7:
                continue
            origin = (z + n_z - s - 1) % n_z if way == 0 else (z + s + 1) % n_z
            landed(loss_all.at[origin], loss_sem.at[way, s])
            if s + 1 < (8 if way == 0 else 7):
                remote(loss_all.at[origin], loss_all.at[origin], loss_sent.at[1],
                       loss_sem.at[way, s + 1], up if way == 0 else down, col)

    st = dict(inv=inv, within=within, carry=carry, read=read, cols=cols, loss=loss)
    for load in more:
        load.wait()
    local = []
    for h in range(2):
        p = slice(h * 128, (h + 1) * 128)
        local.append(
            key_terms(h, q_ref[:, p], x_ref[:, p], ld_ref[h : h + 1, :], wr_ref[h : h + 1, :], st)
        )

    def think():
        for terms in local:
            next(terms, None)

    think()
    think()
    w_step(0)
    think()
    think()
    for i in range(4):
        act_first(i)
    w_step(1)
    think()
    for i in range(4, 8):
        act_first(i)
    w_step(2)
    think()
    w_step(3)
    think()
    think()
    loss_start()
    w_step(4)
    for i in range(4):
        act_second(i)
    loss_first()
    w_step(5)
    for i in range(4, 8):
        act_second(i)
    loss_step(0)
    w_step(6)
    loss_step(1)
    w_step(7)
    loss_step(2)
    act_last()
    loss_step(3)

    total = jnp.zeros((256, 256), f32)
    for k in range(n_z):
        both = jnp.concatenate([act_all[0, k // 2, k % 2], act_all[1, k // 2, k % 2]], axis=0)
        total = total + dot(both, w_all[k], NN)
    part[0] = total[:128]
    part[1] = total[128:]
    remote(part.at[1 - a], part_in, part_sem.at[0], part_sem.at[1], other, col)
    loss_step(4)
    landed(part_in, part_sem.at[1])
    v_ref[...] = (part[a] + part_in[...]).astype(bf16)
    loss_step(5)

    lane_rows = pl.ds(pl.multiple_of(slot * 16, 16), 16)

    def deal(src, dst, send_sem, recv_sem):
        for j in range(16):
            k = (a * 8 + slot + j) % 16
            block = src.at[k // 8, pl.ds(pl.multiple_of((k % 8) * 16, 16), 16), :]
            to = (k // 8) * n_z + (k % 8) * 2
            if j:
                remote(block, dst.at[me], send_sem, recv_sem, to, col)
            else:
                @pl.when(worker)
                def _():
                    pltpu.make_async_copy(block, dst.at[me], recv_sem).start()

                @pl.when(jnp.logical_not(worker))
                def _():
                    remote(block, dst.at[me], send_sem, recv_sem, to, col)

    def give_back(i, src, dst, send_sem, recv_sem):
        mine = i == me
        remote(
            src.at[i], dst.at[jnp.where(mine, 2, a), lane_rows, :], send_sem, recv_sem,
            jnp.where(mine, other, i), col,
        )

    for h in range(2):
        p = slice(h * 128, (h + 1) * 128)
        c = cols[h]
        rs, tail = c[:, 0:1], c[:, 2:3]
        u = dot_left(inv[h] * wr_ref[h : h + 1, :], v_ref[:, p], NN)
        fresh[h] = u
        add[h] = dot_left(u * (tail * rs), x_ref[:, p], TN).astype(bf16)

    deal(add, got, s_send, s_recv)
    loss_step(6)
    loss_step(7)

    @pl.when(worker)
    def _():
        landed(got, s_recv)

        def step(i, s):
            s_low = s.astype(bf16)
            sent[i] = s_low
            give_back(i, sent, state, b_send, b_recv)
            return s - dot(s_low, loss_all[i % 16, i // 16], NN) + got[i].astype(f32)

        lax.fori_loop(0, n_row, step, jnp.zeros((16, 128), f32), unroll=UNROLL)
        state[a, lane_rows, :] = sent[me]

    landed(state.at[pl.ds(0, 2)], b_recv)

    gain = gain_ref[0:1, :]
    for h in range(2):
        p = slice(h * 128, (h + 1) * 128)
        c = cols[h]
        decay = c[:, 1:2]
        s = state[h]
        u = fresh[h] - dot_left(carry[h], s, NT)
        fresh[h] = u
        raw = decay * dot(q_ref[:, p], s, NT) + dot_both(read[h], u, NN)
        r = lax.rsqrt(jnp.mean(raw * raw, axis=1, keepdims=True) + 1e-06)
        out_ref[:, p] = (raw * r * gain).astype(bf16)
        gg = og_ref[:, p].astype(f32) * gain
        d_raw = r * gg - raw * (r * r * r * jnp.mean(raw * gg, axis=1, keepdims=True))
        grad_raw[h] = d_raw
        back = dot_both(read[h], d_raw, TN)
        summed[h] = back
        add2[h] = (dot_left(decay * d_raw, q_ref[:, p], TN) - dot_both(back, carry[h], TN)).astype(bf16)

    deal(add2, got2, t_send, t_recv)

    @pl.when(worker)
    def _():
        landed(got2, t_recv)

        def step(k, s):
            i = n_row - 1 - k
            s_low = s.astype(bf16)
            sent2[i] = s_low
            give_back(i, sent2, grad, u_send, u_recv)
            return s - dot(s_low, loss_all[i % 16, i // 16], NT) + got2[i].astype(f32)

        lax.fori_loop(0, n_row, step, jnp.zeros((16, 128), f32), unroll=UNROLL)
        grad[a, lane_rows, :] = sent2[me]

    landed(grad.at[pl.ds(0, 2)], u_recv)

    n = 128
    rows_i = lax.broadcasted_iota(jnp.int32, (n, n), 0)
    cols_i = lax.broadcasted_iota(jnp.int32, (n, n), 1)
    own_tokens = pl.ds(pl.multiple_of(a * 128, 128), 128)
    later = []
    for h in range(2):
        p = slice(h * 128, (h + 1) * 128)
        c = cols[h]
        rs, tail, b = c[:, 0:1], c[:, 2:3], c[:, 3:4]
        d_u = summed[h] + (tail * rs) * dot(x_ref[:, p], grad[h], NT)
        grown = dot_both(inv[h], d_u, TN)
        later.append(grown)
        dv_all[own_tokens, p] = (b * grown).astype(bf16)
    mine = dv_all.at[own_tokens, :]
    remote(mine, mine, dv_sem.at[0], dv_sem.at[1], other, col)

    def query_key_grads(h):
        p = slice(h * 128, (h + 1) * 128)
        q, x = q_ref[:, p], x_ref[:, p]
        c = cols[h]
        rs, decay, tail, b = c[:, 0:1], c[:, 1:2], c[:, 2:3], c[:, 3:4]
        s, g, u, d_raw, grown = state[h], grad[h], fresh[h], grad_raw[h], later[h]
        rs_row = jnp.sum(jnp.where(rows_i == cols_i, rs, 0.0), axis=0, keepdims=True)
        d_read = dot_both(d_raw, u, NT) * within[h]
        dq_ref[:, p] = (decay * dot_left(d_raw, s, NN) + dot_left(d_read * rs_row, x, NN)).astype(bf16)
        d_gram = jnp.where(rows_i > cols_i, -b * within[h] * dot_both(grown, u, NT), 0.0)
        d_k = (
            dot_left(d_read, q, TN)
            + tail * dot_left(u, g, NN)
            - (b * decay) * dot_left(grown, s, NN)
            + dot_left(d_gram * rs_row, x, NN)
            + dot_left(d_gram * rs, x, TN)
        )
        unit = rs * x.astype(f32)
        dk_ref[:, p] = (rs * (d_k - unit * jnp.sum(unit * d_k, axis=1, keepdims=True))).astype(bf16)

    theirs = dv_all.at[pl.ds(pl.multiple_of((1 - a) * 128, 128), 128), :]
    landed(theirs, dv_sem.at[1])

    def w_term(d):
        acc = dot(act_all[0, d // 2, d % 2], dv_all[0:128, :], TN)
        return acc + dot(act_all[1, d // 2, d % 2], dv_all[128:256, :], TN)

    def r_dest(s, way):
        return (z + 8 - s) % n_z if way == 0 else (z + n_z - 7 + s) % n_z

    def r_slot(s, way):
        return w_right.at[s] if way == 0 else w_left.at[s]

    def r_send(s, way):
        d = r_dest(s, way)
        for sub in range(SUBS):
            q = pl.ds(sub * SUB, SUB)
            if s > 0:
                landed(r_slot(s - 1, way).at[q, :], r_sem.at[way, s - 1, sub])
                w_terms[d, q, :] = (
                    w_terms[d, q, :].astype(f32) + r_slot(s - 1, way)[q, :].astype(f32)
                ).astype(bf16)
            remote(w_terms.at[d, q, :], r_slot(s, way).at[q, :], r_sent, r_sem.at[way, s, sub],
                   up if way == 0 else down, col)

    def r_make(s):
        for way in range(2):
            if way == 1 and s == 7:
                continue
            d = r_dest(s, way)
            w_terms[d] = w_term(d).astype(bf16)

    def r_step(s):
        for way in range(2):
            if way == 1 and s == 7:
                continue
            r_send(s, way)

    def in_make(cc):
        for i in range(2):
            both = dot(dv_all[...], w_all[cc * 2 + i], NT).astype(bf16)
            for t in range(2):
                in_terms[t, cc, i] = both[t * 128 : (t + 1) * 128]

    def plus(t, cc, f, ref):
        in_terms[t, cc, f] = (in_terms[t, cc, f].astype(f32) + ref[...].astype(f32)).astype(bf16)

    def sib_send(k):
        cc = k * 2 + 1 - core
        in_make(cc)
        for t in range(2):
            for f in range(2):
                remote(in_terms.at[t, cc, f], in_sib.at[t, k, f], i_sent, sib_sem.at[t, k, f], me, twin)

    def own_make(k):
        in_make(k * 2 + core)

    def near_send(i):
        t, xh, f = i // 4, (i // 2) % 2, i % 2
        k = (1 - first) * 2 + xh
        cc = k * 2 + core
        landed(in_sib.at[t, k, f], sib_sem.at[t, k, f])
        plus(t, cc, f, in_sib.at[t, k, f])
        remote(in_terms.at[t, cc, f], in_near.at[t, xh, f], i_sent, near_sem.at[t, xh, f], me, col_near)

    def far_send(i):
        t, xh, f = i // 4, (i // 2) % 2, i % 2
        k = first * 2 + xh
        cc = k * 2 + core
        landed(in_sib.at[t, k, f], sib_sem.at[t, k, f])
        plus(t, cc, f, in_sib.at[t, k, f])
        landed(in_near.at[t, xh, f], near_sem.at[t, xh, f])
        plus(t, cc, f, in_near.at[t, xh, f])

        @pl.when(jnp.logical_not(source))
        def _():
            remote(in_terms.at[t, cc, f], in_far.at[t, xh, f], i_sent, far_sem.at[t, xh, f], me, col_far)

    def home_send(i):
        t, xh, f = i // 4, (i // 2) % 2, i % 2
        k = first * 2 + xh
        cc = k * 2 + core

        @pl.when(source)
        def _():
            landed(in_far.at[t, xh, f], far_sem.at[t, xh, f])
            plus(t, cc, f, in_far.at[t, xh, f])
            row_to, col_to = t * n_z + z, y * 4 + xh * 2 + core
            here = (row_to == me) & (col_to == col)
            dst, sem = in_last.at[x_hi, f], last_sem.at[x_hi, f]

            @pl.when(jnp.logical_not(here))
            def _():
                remote(in_terms.at[t, cc, f], dst, i_sent, sem, row_to, col_to)

            @pl.when(here)
            def _():
                pltpu.make_async_copy(in_terms.at[t, cc, f], dst, sem).start()

    r_make(0)
    r_step(0)
    for k in range(4):
        sib_send(k)
    r_make(1)
    for k in range(4):
        own_make(k)
    r_step(1)
    r_make(2)
    for i in range(4):
        near_send(i)
    r_step(2)
    for i in range(4, 8):
        near_send(i)
    r_make(3)
    query_key_grads(0)
    r_step(3)
    r_make(4)
    for i in range(4):
        far_send(i)
    r_step(4)
    r_make(5)
    for i in range(4, 8):
        far_send(i)
    query_key_grads(1)
    r_step(5)
    r_make(6)
    for i in range(4):
        home_send(i)
    r_step(6)
    r_make(7)
    for i in range(4, 8):
        home_send(i)
    r_step(7)
    own_term = w_term(z)
    for xh in range(2):
        for f in range(2):
            landed(in_last.at[xh, f], last_sem.at[xh, f])
    for i in range(2):
        din_ref[:, i * 256 : (i + 1) * 256] = (
            in_last[0, i].astype(f32) + in_last[1, i].astype(f32)
        ).astype(bf16)
    for sub in range(SUBS):
        q = pl.ds(sub * SUB, SUB)
        landed(w_right.at[7, q, :], r_sem.at[0, 7, sub])
        landed(w_left.at[6, q, :], r_sem.at[1, 6, sub])
    dw_ref[...] = own_term + w_right[7].astype(f32) + w_left[6].astype(f32)

    def drain(ref, count, sem):
        def one(i, _):
            pltpu.make_async_copy(ref, ref, sem).wait()
            return 0
        lax.fori_loop(0, count, one, 0)

    big = act_own.at[0]
    own = jnp.where(worker, 1, 0)
    far = jnp.where(source, 1, 0)
    self_home = jnp.where(source, 1, 0)
    drain(big, (2 - self_home + 4 + 4 * far + 8) * 2, act_sent)
    drain(w_all.at[0, pl.ds(0, SUB), :], 15 * SUBS, w_sent)
    landed(part.at[0], part_sem.at[0])
    landed(loss.at[0], loss_sent.at[0])
    drain(loss_all.at[0], 15, loss_sent.at[1])
    drain(got.at[0], 16 - own, s_send)
    drain(got.at[0], 16 - own, t_send)

    @pl.when(worker)
    def _():
        drain(got.at[0], n_row, b_send)
        drain(got.at[0], n_row, u_send)

    landed(mine, dv_sem.at[0])
    drain(w_all.at[0, pl.ds(0, SUB), :], 15 * SUBS, r_sent)
    drain(big, (8 + 4 + 4 * (1 - far) + (4 - 1) * far) * 2, i_sent)


def layer(act, w, q, x, og, ld, wr, gain):
    sq = (2, 128, 128)
    vm = pl.BlockSpec(memory_space=pltpu.VMEM)
    o = jax.ShapeDtypeStruct((128, 256), bf16)
    dma = pltpu.SemaphoreType.DMA
    V = pltpu.VMEM
    return pl.pallas_call(
        layer_kernel,
        out_shape=(
            o,
            jax.ShapeDtypeStruct((128, 512), bf16),
            o,
            o,
            jax.ShapeDtypeStruct((256, 256), f32),
        ),
        in_specs=[pl.BlockSpec(memory_space=pl.ANY)] * 8,
        out_specs=(vm,) * 5,
        scratch_shapes=[
            V(sq, f32), V(sq, f32), V(sq, f32), V(sq, f32), V(sq, f32), V(sq, bf16),
            V(sq, f32), V(sq, f32), V(sq, f32), V((128, 256), bf16),
            V((2, 128, 256), bf16), V((2, 8, 2, 128, 256), bf16), V((16, 256, 256), bf16),
            V((2, 128, 256), f32), V((128, 256), f32), V((16, 2, 128, 128), bf16),
            V(sq, bf16), V(sq, bf16), V((32, 16, 128), bf16), V((32, 16, 128), bf16),
            V((32, 16, 128), bf16), V((32, 16, 128), bf16), V((3, 128, 128), bf16), V((3, 128, 128), bf16),
            V((256, 256), bf16), V((16, 256, 256), bf16), V((8, 256, 256), bf16),
            V((7, 256, 256), bf16), V((2, 8, 2, 128, 256), bf16), V((2, 4, 2, 128, 256), bf16),
            V((2, 2, 2, 128, 256), bf16), V((2, 2, 2, 128, 256), bf16), V((2, 2, 128, 256), bf16),
            dma((2, 8, 2)), dma, dma((2, 8, SUBS)), dma, dma((2,)), dma((3, 8)), dma((2,)),
            dma, dma, dma, dma, dma, dma, dma, dma,
            dma((2,)), dma((2, 8, SUBS)), dma, dma, dma((2, 4, 2)), dma((2, 2, 2)), dma((2, 2, 2)), dma((2, 2)),
            V((128, 256), bf16), V((128, 256), bf16), V((128, 256), bf16), V((2, 128), f32),
            V((2, 128), f32), V((1, 128), f32), dma((9,)),
        ],
        compiler_params=pltpu.CompilerParams(
            collective_id=1, has_side_effects=True, vmem_limit_bytes=48 * 1024 * 1024
        ),
        name="layer",
    )(act, w, q, x, og, ld, wr, gain)


def shards(
    activations, w_value, query_input, key_input, log_decay, write_rate, norm_gain, out_grad
):
    return layer(
        activations, w_value, query_input, key_input, out_grad, log_decay, write_rate,
        norm_gain.reshape(1, -1),
    )


def solution(mesh):
    split = P("row", "col")
    flipped = P("col", "row")
    return jax.shard_map(
        shards,
        mesh=mesh,
        in_specs=(split, split, split, split, flipped, flipped, P(), split),
        out_specs=(split,) * 5,
        check_vma=False,
    )
```

```python
import functools

import jax
import jax.numpy as jnp
from jax import lax
from jax.experimental import pallas as pl
from jax.experimental.pallas import tpu as pltpu
from jax.sharding import PartitionSpec as P

MESH = pl.DeviceIdType.MESH
f32 = jnp.float32
bf16 = jnp.bfloat16
NN = (((1,), (0,)), ((), ()))
NT = (((1,), (1,)), ((), ()))
TN = (((0,), (0,)), ((), ()))


def dot(a, b, dims):
    return lax.dot_general(a, b, dims, preferred_element_type=f32)


def halves(a):
    high = a.astype(bf16)
    return high, (a - high.astype(f32)).astype(bf16)


def dot_left(a, b, dims):
    high, low = halves(a)
    return dot(high, b, dims) + dot(low, b, dims)


def dot_both(a, b, dims):
    a_high, a_low = halves(a)
    b_high, b_low = halves(b)
    return dot(a_high, b_high, dims) + (dot(a_high, b_low, dims) + dot(a_low, b_high, dims))


def key_terms(h, q, x, ld, wr, st):
    n = x.shape[0]
    rows = lax.broadcasted_iota(jnp.int32, (n, n), 0)
    cols = lax.broadcasted_iota(jnp.int32, (n, n), 1)
    lower = rows >= cols
    strict = rows > cols
    eye = rows == cols

    def col_of(row):
        return jnp.sum(jnp.where(eye, row, 0.0), axis=1, keepdims=True)

    def row_of(col):
        return jnp.sum(jnp.where(eye, col, 0.0), axis=0, keepdims=True)

    xf = x.astype(f32)
    rs = lax.rsqrt(jnp.sum(xf * xf, axis=1, keepdims=True) + 1e-06)
    rs_row = row_of(rs)
    g = jnp.sum(jnp.where(lower, ld, 0.0), axis=1, keepdims=True)
    g_row = row_of(g)
    total = jnp.sum(ld, axis=1, keepdims=True)
    decay = jnp.exp(g)
    decay_row = jnp.exp(g_row)
    tail = jnp.exp(total - g)
    b = col_of(wr)
    within = jnp.where(lower, jnp.exp(jnp.where(lower, g - g_row, 0.0)), 0.0)
    gram = dot(x, x, NT) * (rs * rs_row)
    coupling = jnp.where(strict, b * within * gram, 0.0)
    ident = jnp.where(eye, 1.0, 0.0)
    near = jnp.where((rows // 16) == (cols // 16), coupling, 0.0)
    inv = ident - near
    power = near
    yield
    for _ in range(3):
        power = dot_both(power, power, NN)
        inv = inv + dot_both(inv, power, NN)
        yield
    size = 16
    while size < n:
        off = ((rows // (2 * size)) == (cols // (2 * size))) & ((rows // size) != (cols // size))
        part = jnp.where(off, coupling, 0.0)
        inv = inv - dot_both(dot_both(inv, part, NN), inv, NN)
        size *= 2
        yield
    st["inv"][h] = inv
    st["within"][h] = within
    carry = dot_left(inv * (wr * decay_row * rs_row), x, NN)
    read = dot(q, x, NT) * within * rs_row
    loss = dot_left(carry * (tail * rs), x, TN) + jnp.where(eye, 1.0 - jnp.exp(total), 0.0)
    st["carry"][h] = carry
    st["read"][h] = read
    lanes = jnp.zeros((n, 128), f32)
    lane = lax.broadcasted_iota(jnp.int32, (n, 128), 1)
    for i, c in enumerate((rs, decay, tail, b)):
        lanes = jnp.where(lane == i, c, lanes)
    st["cols"][h] = lanes
    st["loss"][h] = loss.astype(bf16)


SUBS = 4
UNROLL = 4
FIRST = 3
ORDER = (
    "t", "w0", "a0123", "t", "w1", "a4567", "t", "t", "t", "s", "w2", "c01", "b01", "p",
    "w3", "b234", "c234", "l0", "w4", "b567", "c567", "l1", "w5", "d0123", "l2",
    "w6", "d4567", "l3", "w7", "x", "l4",
)
SUB = 256 // SUBS
R_SUBS = 4
R_SUB = 256 // R_SUBS


def layer_kernel(
    act_hbm, w_hbm, q_hbm, x_hbm, og_hbm, ld_hbm, wr_hbm, gain_hbm,
    out_ref, din_ref, dq_ref, dk_ref, dw_ref,
    inv, within, carry, read, cols, loss, fresh, grad_raw, summed, v_ref,
    act_own, act_all, w_all, part, part_in, loss_all,
    add, add2, got, got2, sent, sent2, state, grad,
    dv_all, w_terms, w_right, w_left, in_terms, in_sib, in_near, in_far, in_last,
    act_sem, act_sent, w_sem, w_sent, part_sem, loss_sem, loss_sent,
    s_send, s_recv, b_send, b_recv, t_send, t_recv, u_send, u_recv,
    dv_sem, r_sem, r_sent, i_sent, sib_sem, near_sem, far_sem, last_sem,
    q_ref, x_ref, og_ref, ld_ref, wr_ref, gain_ref, load_sem,
):
    n_row, n_z = 32, 16
    me, col = lax.axis_index("row"), lax.axis_index("col")
    a, z = me // n_z, me % n_z
    other = (1 - a) * n_z + z
    y, x_hi, core = col // 4, (col // 2) % 2, col % 2
    twin = col + 1 - 2 * core
    y_near = y + 1 - 2 * (y % 2)
    col_near = y_near * 4 + x_hi * 2 + core
    col_far = (3 - y) * 4 + x_hi * 2 + core
    source = a == y // 2
    first = jnp.where(source, y % 2, 1 - y % 2)
    slot = z // 2
    worker = z % 2 == 0
    up, down = a * n_z + (z + 1) % n_z, a * n_z + (z + n_z - 1) % n_z

    barrier = pltpu.get_barrier_semaphore()

    col_side = y * 4 + (1 - x_hi) * 2 + core
    for row_to, col_to in (
        (up, col), (down, col), (other, col), (me, twin), (me, col_near), (me, col_far),
        (me, col_side), (other, col_side),
    ):
        pl.semaphore_signal(barrier, inc=1, device_id=(row_to, col_to), device_id_type=MESH)
    w_own = w_all.at[z]
    loads = [
        pltpu.make_async_copy(act_hbm.at[:, pl.ds(i * 256, 256)], act_own.at[i], load_sem.at[i])
        for i in range(2)
    ] + [pltpu.make_async_copy(w_hbm, w_own, load_sem.at[2])]
    more = [
        pltpu.make_async_copy(src, dst, load_sem.at[3 + i])
        for i, (src, dst) in enumerate((
            (q_hbm, q_ref), (x_hbm, x_ref), (og_hbm, og_ref), (ld_hbm, ld_ref), (wr_hbm, wr_ref),
            (gain_hbm, gain_ref),
        ))
    ]
    for load in more + loads:
        load.start()

    st = dict(inv=inv, within=within, carry=carry, read=read, cols=cols, loss=loss)
    for load in more:
        load.wait()
    local = []
    for h in range(2):
        p = slice(h * 128, (h + 1) * 128)
        local.append(
            key_terms(h, q_ref[:, p], x_ref[:, p], ld_ref[h : h + 1, :], wr_ref[h : h + 1, :], st)
        )

    def think():
        for terms in local:
            next(terms, None)

    for _ in range(FIRST):
        think()
    for load in loads:
        load.wait()
    pl.semaphore_wait(barrier, 8)

    def remote(src, dst, send_sem, recv_sem, row_to, col_to):
        pltpu.make_async_remote_copy(
            src_ref=src, dst_ref=dst, send_sem=send_sem, recv_sem=recv_sem,
            device_id=(row_to, col_to), device_id_type=MESH,
        ).start()

    def landed(ref, sem):
        pltpu.make_async_copy(ref, ref, sem).wait()

    home_row = (y // 2) * n_z + z
    for xh in range(2):
        to_col = y * 4 + xh * 2 + core
        here = source & (x_hi == xh)
        for f in range(2):
            dst, sem = act_all.at[a, col % 8, f], act_sem.at[a, col % 8, f]

            @pl.when(jnp.logical_not(here))
            def _():
                remote(act_own.at[f], dst, act_sent, sem, home_row, to_col)

            @pl.when(here)
            def _():
                pltpu.make_async_copy(act_own.at[f], dst, sem).start()

    def act_first(i, is_source):
        t, xh, f = i // 4, (i // 2) % 2, i % 2
        cc = first * 4 + xh * 2 + core
        ref, sem = act_all.at[t, cc, f], act_sem.at[t, cc, f]
        landed(ref, sem)

        if is_source:
            remote(ref, ref, act_sent, sem, me, col_far)
        remote(ref, ref, act_sent, sem, me, col_near)
        remote(ref, ref, act_sent, sem, me, twin)

    def act_second(i):
        t, xh, f = i // 4, (i // 2) % 2, i % 2
        cc = (1 - first) * 4 + xh * 2 + core
        ref, sem = act_all.at[t, cc, f], act_sem.at[t, cc, f]
        landed(ref, sem)
        remote(ref, ref, act_sent, sem, me, twin)

    def act_last():
        for t in range(2):
            for k in range(4):
                cc = k * 2 + (1 - core)
                for f in range(2):
                    landed(act_all.at[t, cc, f], act_sem.at[t, cc, f])

    def w_piece(s, way, sub, origin):
        ref = w_all.at[origin, pl.ds(sub * SUB, SUB), :]
        return ref, w_sem.at[way, s, sub]

    def w_send(s, way):
        origin = (z + n_z - s) % n_z if way == 0 else (z + s) % n_z
        for sub in range(SUBS):
            ref, sem = w_piece(s, way, sub, origin)
            remote(ref, ref, w_sent, sem, up if way == 0 else down, col)

    def w_step(s):
        for sub in range(SUBS):
            for way in range(2):
                if way == 1 and s == 7:
                    continue
                origin = (z + n_z - s - 1) % n_z if way == 0 else (z + s + 1) % n_z
                ref, sem = w_piece(s, way, sub, origin)
                landed(ref, sem)
                if s + 1 < (8 if way == 0 else 7):
                    _, after = w_piece(s + 1, way, sub, origin)
                    remote(ref, ref, w_sent, after, up if way == 0 else down, col)

    w_send(0, 0)
    w_send(0, 1)

    def loss_send(k, s):
        for way in range(2):
            if s >= (8 if way == 0 else 7):
                continue
            origin = (z + n_z - s) % n_z if way == 0 else (z + s) % n_z
            owner = a if k == 0 else 1 - a
            ref = loss_all.at[origin, owner]
            remote(ref, ref, loss_sent.at[1], loss_sem.at[way, s, owner], up if way == 0 else down, col)

    def loss_start():
        remote(loss.at[1 - a], loss_all.at[z, a], loss_sent.at[0], loss_sem.at[2, 0, 0], other, col)
        loss_all[z, a] = loss[a]
        loss_send(0, 0)

    def loss_first():
        landed(loss_all.at[z, 1 - a], loss_sem.at[2, 0, 0])
        loss_send(1, 0)

    def loss_step(s):
        for k in range(2):
            owner = a if k == 0 else 1 - a
            for way in range(2):
                if way == 1 and s == 7:
                    continue
                origin = (z + n_z - s - 1) % n_z if way == 0 else (z + s + 1) % n_z
                landed(loss_all.at[origin, owner], loss_sem.at[way, s, owner])
            loss_send(k, s + 1)

    def at_source(work):
        pl.when(source)(work)

    def at_sink(work):
        pl.when(jnp.logical_not(source))(work)

    def each(work, numbers, *rest):
        for number in numbers:
            work(int(number), *rest)

    for item in ORDER:
        what, number = item[0], item[1:]
        if what == "t":
            think()
        elif what == "w":
            w_step(int(number))
        elif what == "a":
            at_source(functools.partial(each, act_first, number, True))
        elif what == "b":
            at_sink(functools.partial(each, act_first, number, False))
        elif what == "c":
            at_source(functools.partial(each, act_second, number))
        elif what == "d":
            at_sink(functools.partial(each, act_second, number))
        elif what == "s":
            loss_start()
        elif what == "p":
            loss_first()
        elif what == "l":
            loss_step(int(number))
        elif what == "x":
            act_last()

    total = jnp.zeros((256, 256), f32)
    for k in range(n_z):
        both = jnp.concatenate([act_all[0, k // 2, k % 2], act_all[1, k // 2, k % 2]], axis=0)
        total = total + dot(both, w_all[k], NN)
    part[0] = total[:128]
    part[1] = total[128:]
    remote(part.at[1 - a], part_in, part_sem.at[0], part_sem.at[1], other, col)
    landed(part_in, part_sem.at[1])
    v_ref[...] = (part[a] + part_in[...]).astype(bf16)
    loss_step(5)

    lane_rows = pl.ds(pl.multiple_of(slot * 16, 16), 16)

    def deal(src, dst, send_sem, recv_sem):
        for j in (4, 12, 5, 13, 3, 11, 6, 14, 2, 10, 7, 15, 1, 9, 8, 0):
            k = (1 - a + j // 8) % 2 * 8 + (slot + j) % 8
            block = src.at[k // 8, pl.ds(pl.multiple_of((k % 8) * 16, 16), 16), :]
            to = (k // 8) * n_z + (k % 8) * 2
            if j != 8:
                remote(block, dst.at[me], send_sem, recv_sem.at[me], to, col)
            else:
                @pl.when(worker)
                def _():
                    pltpu.make_async_copy(block, dst.at[me], recv_sem.at[me]).start()

                @pl.when(jnp.logical_not(worker))
                def _():
                    remote(block, dst.at[me], send_sem, recv_sem.at[me], to, col)

    def give_back(i, src, dst, send_sem, recv_sem):
        mine = i == me
        remote(
            src.at[i], dst.at[jnp.where(mine, 2, a), lane_rows, :], send_sem, recv_sem,
            jnp.where(mine, other, i), col,
        )

    for h in range(2):
        p = slice(h * 128, (h + 1) * 128)
        c = cols[h]
        rs, tail = c[:, 0:1], c[:, 2:3]
        u = dot_left(inv[h] * wr_ref[h : h + 1, :], v_ref[:, p], NN)
        fresh[h] = u
        add[h] = dot_left(u * (tail * rs), x_ref[:, p], TN).astype(bf16)

    deal(add, got, s_send, s_recv)
    loss_step(6)
    loss_step(7)

    @pl.when(worker)
    def _():
        def step(i, s):
            s_low = s.astype(bf16)
            sent[i] = s_low
            give_back(i, sent, state, b_send, b_recv)
            landed(got.at[i], s_recv.at[i])
            return s - dot(s_low, loss_all[i % 16, i // 16], NN) + got[i].astype(f32)

        lax.fori_loop(0, n_row, step, jnp.zeros((16, 128), f32), unroll=UNROLL)
        state[a, lane_rows, :] = sent[me]

    landed(state.at[pl.ds(0, 2)], b_recv)

    gain = gain_ref[0:1, :]
    for h in range(2):
        p = slice(h * 128, (h + 1) * 128)
        c = cols[h]
        decay = c[:, 1:2]
        s = state[h]
        u = fresh[h] - dot_left(carry[h], s, NT)
        fresh[h] = u
        raw = decay * dot(q_ref[:, p], s, NT) + dot_both(read[h], u, NN)
        r = lax.rsqrt(jnp.mean(raw * raw, axis=1, keepdims=True) + 1e-06)
        out_ref[:, p] = (raw * r * gain).astype(bf16)
        gg = og_ref[:, p].astype(f32) * gain
        d_raw = r * gg - raw * (r * r * r * jnp.mean(raw * gg, axis=1, keepdims=True))
        grad_raw[h] = d_raw
        back = dot_both(read[h], d_raw, TN)
        summed[h] = back
        add2[h] = (dot_left(decay * d_raw, q_ref[:, p], TN) - dot_both(back, carry[h], TN)).astype(bf16)

    deal(add2, got2, t_send, t_recv)

    @pl.when(worker)
    def _():
        def step(k, s):
            i = n_row - 1 - k
            s_low = s.astype(bf16)
            sent2[i] = s_low
            give_back(i, sent2, grad, u_send, u_recv)
            landed(got2.at[i], t_recv.at[i])
            return s - dot(s_low, loss_all[i % 16, i // 16], NT) + got2[i].astype(f32)

        lax.fori_loop(0, n_row, step, jnp.zeros((16, 128), f32), unroll=UNROLL)
        grad[a, lane_rows, :] = sent2[me]

    landed(grad.at[pl.ds(0, 2)], u_recv)

    n = 128
    rows_i = lax.broadcasted_iota(jnp.int32, (n, n), 0)
    cols_i = lax.broadcasted_iota(jnp.int32, (n, n), 1)
    own_tokens = pl.ds(pl.multiple_of(a * 128, 128), 128)
    later = []
    for h in range(2):
        p = slice(h * 128, (h + 1) * 128)
        c = cols[h]
        rs, tail, b = c[:, 0:1], c[:, 2:3], c[:, 3:4]
        d_u = summed[h] + (tail * rs) * dot(x_ref[:, p], grad[h], NT)
        grown = dot_both(inv[h], d_u, TN)
        later.append(grown)
        dv_all[own_tokens, p] = (b * grown).astype(bf16)
    mine = dv_all.at[own_tokens, :]
    remote(mine, mine, dv_sem.at[0], dv_sem.at[1], other, col)

    def query_key_grads(h):
        p = slice(h * 128, (h + 1) * 128)
        q, x = q_ref[:, p], x_ref[:, p]
        c = cols[h]
        rs, decay, tail, b = c[:, 0:1], c[:, 1:2], c[:, 2:3], c[:, 3:4]
        s, g, u, d_raw, grown = state[h], grad[h], fresh[h], grad_raw[h], later[h]
        rs_row = jnp.sum(jnp.where(rows_i == cols_i, rs, 0.0), axis=0, keepdims=True)
        d_read = dot_both(d_raw, u, NT) * within[h]
        dq_ref[:, p] = (decay * dot_left(d_raw, s, NN) + dot_left(d_read * rs_row, x, NN)).astype(bf16)
        d_gram = jnp.where(rows_i > cols_i, -b * within[h] * dot_both(grown, u, NT), 0.0)
        d_k = (
            dot_left(d_read, q, TN)
            + tail * dot_left(u, g, NN)
            - (b * decay) * dot_left(grown, s, NN)
            + dot_left(d_gram * rs_row, x, NN)
            + dot_left(d_gram * rs, x, TN)
        )
        unit = rs * x.astype(f32)
        dk_ref[:, p] = (rs * (d_k - unit * jnp.sum(unit * d_k, axis=1, keepdims=True))).astype(bf16)

    theirs = dv_all.at[pl.ds(pl.multiple_of((1 - a) * 128, 128), 128), :]
    landed(theirs, dv_sem.at[1])

    def w_term(d):
        acc = dot(act_all[0, d // 2, d % 2], dv_all[0:128, :], TN)
        return acc + dot(act_all[1, d // 2, d % 2], dv_all[128:256, :], TN)

    def r_dest(s, way):
        return (z + 8 - s) % n_z if way == 0 else (z + n_z - 7 + s) % n_z

    def r_slot(s, way):
        return w_right.at[s] if way == 0 else w_left.at[s]

    def r_send(s, way):
        d = r_dest(s, way)
        for sub in range(R_SUBS):
            q = pl.ds(sub * R_SUB, R_SUB)
            if s > 0:
                landed(r_slot(s - 1, way).at[q, :], r_sem.at[way, s - 1, sub])
                w_terms[d, q, :] = (
                    w_terms[d, q, :].astype(f32) + r_slot(s - 1, way)[q, :].astype(f32)
                ).astype(bf16)
            remote(w_terms.at[d, q, :], r_slot(s, way).at[q, :], r_sent, r_sem.at[way, s, sub],
                   up if way == 0 else down, col)

    def r_make(s):
        for way in range(2):
            if way == 1 and s == 7:
                continue
            d = r_dest(s, way)
            w_terms[d] = w_term(d).astype(bf16)

    def r_step(s):
        for way in range(2):
            if way == 1 and s == 7:
                continue
            r_send(s, way)

    def in_make(cc):
        for i in range(2):
            both = dot(dv_all[...], w_all[cc * 2 + i], NT).astype(bf16)
            for t in range(2):
                in_terms[t, cc, i] = both[t * 128 : (t + 1) * 128]

    def plus(t, cc, f, ref):
        in_terms[t, cc, f] = (in_terms[t, cc, f].astype(f32) + ref[...].astype(f32)).astype(bf16)

    def sib_send(k):
        cc = k * 2 + 1 - core
        in_make(cc)
        for t in range(2):
            for f in range(2):
                remote(in_terms.at[t, cc, f], in_sib.at[t, k, f], i_sent, sib_sem.at[t, k, f], me, twin)

    def own_make(k):
        in_make(k * 2 + core)

    def near_send(i):
        t, xh, f = i // 4, (i // 2) % 2, i % 2
        k = (1 - first) * 2 + xh
        cc = k * 2 + core
        landed(in_sib.at[t, k, f], sib_sem.at[t, k, f])
        plus(t, cc, f, in_sib.at[t, k, f])
        remote(in_terms.at[t, cc, f], in_near.at[t, xh, f], i_sent, near_sem.at[t, xh, f], me, col_near)

    def far_send(i):
        t, xh, f = i // 4, (i // 2) % 2, i % 2
        k = first * 2 + xh
        cc = k * 2 + core
        landed(in_sib.at[t, k, f], sib_sem.at[t, k, f])
        plus(t, cc, f, in_sib.at[t, k, f])
        landed(in_near.at[t, xh, f], near_sem.at[t, xh, f])
        plus(t, cc, f, in_near.at[t, xh, f])

        @pl.when(jnp.logical_not(source))
        def _():
            remote(in_terms.at[t, cc, f], in_far.at[t, xh, f], i_sent, far_sem.at[t, xh, f], me, col_far)

    def home_send(i):
        t, xh, f = i // 4, (i // 2) % 2, i % 2
        k = first * 2 + xh
        cc = k * 2 + core

        @pl.when(source)
        def _():
            landed(in_far.at[t, xh, f], far_sem.at[t, xh, f])
            plus(t, cc, f, in_far.at[t, xh, f])
            row_to, col_to = t * n_z + z, y * 4 + xh * 2 + core
            here = (row_to == me) & (col_to == col)
            dst, sem = in_last.at[x_hi, f], last_sem.at[x_hi, f]

            @pl.when(jnp.logical_not(here))
            def _():
                remote(in_terms.at[t, cc, f], dst, i_sent, sem, row_to, col_to)

            @pl.when(here)
            def _():
                pltpu.make_async_copy(in_terms.at[t, cc, f], dst, sem).start()

    r_make(0)
    r_step(0)
    for k in range(4):
        sib_send(k)
    r_make(1)
    for k in range(4):
        own_make(k)
    r_step(1)
    r_make(2)
    for i in range(4):
        near_send(i)
    r_step(2)
    for i in range(4, 8):
        near_send(i)
    r_make(3)
    query_key_grads(0)
    r_step(3)
    r_make(4)
    for i in range(4):
        far_send(i)
    r_step(4)
    r_make(5)
    for i in range(4, 8):
        far_send(i)
    query_key_grads(1)
    r_step(5)
    r_make(6)
    for i in range(4):
        home_send(i)
    r_step(6)
    r_make(7)
    for i in range(4, 8):
        home_send(i)
    r_step(7)
    own_term = w_term(z)
    for xh in range(2):
        for f in range(2):
            landed(in_last.at[xh, f], last_sem.at[xh, f])
    for i in range(2):
        din_ref[:, i * 256 : (i + 1) * 256] = (
            in_last[0, i].astype(f32) + in_last[1, i].astype(f32)
        ).astype(bf16)
    for sub in range(R_SUBS):
        q = pl.ds(sub * R_SUB, R_SUB)
        landed(w_right.at[7, q, :], r_sem.at[0, 7, sub])
        landed(w_left.at[6, q, :], r_sem.at[1, 6, sub])
    dw_ref[...] = own_term + w_right[7].astype(f32) + w_left[6].astype(f32)

    def drain(ref, count, sem):
        def one(i, _):
            pltpu.make_async_copy(ref, ref, sem).wait()
            return 0
        lax.fori_loop(0, count, one, 0)

    big = act_own.at[0]
    own = jnp.where(worker, 1, 0)
    far = jnp.where(source, 1, 0)
    self_home = jnp.where(source, 1, 0)
    drain(big, (2 - self_home + 4 + 4 * far + 8) * 2, act_sent)
    drain(w_all.at[0, pl.ds(0, SUB), :], 15 * SUBS, w_sent)
    landed(part.at[0], part_sem.at[0])
    landed(loss.at[0], loss_sent.at[0])
    drain(loss.at[0], 30, loss_sent.at[1])
    drain(got.at[0], 16 - own, s_send)
    drain(got.at[0], 16 - own, t_send)

    @pl.when(worker)
    def _():
        drain(got.at[0], n_row, b_send)
        drain(got.at[0], n_row, u_send)

    landed(mine, dv_sem.at[0])
    drain(w_all.at[0, pl.ds(0, R_SUB), :], 15 * R_SUBS, r_sent)
    drain(big, (8 + 4 + 4 * (1 - far) + (4 - 1) * far) * 2, i_sent)


def layer(act, w, q, x, og, ld, wr, gain):
    sq = (2, 128, 128)
    vm = pl.BlockSpec(memory_space=pltpu.VMEM)
    o = jax.ShapeDtypeStruct((128, 256), bf16)
    dma = pltpu.SemaphoreType.DMA
    V = pltpu.VMEM
    return pl.pallas_call(
        layer_kernel,
        out_shape=(
            o,
            jax.ShapeDtypeStruct((128, 512), bf16),
            o,
            o,
            jax.ShapeDtypeStruct((256, 256), f32),
        ),
        in_specs=[pl.BlockSpec(memory_space=pltpu.HBM)] * 8,
        out_specs=(vm,) * 5,
        scratch_shapes=[
            V(sq, f32), V(sq, f32), V(sq, f32), V(sq, f32), V(sq, f32), V(sq, bf16),
            V(sq, f32), V(sq, f32), V(sq, f32), V((128, 256), bf16),
            V((2, 128, 256), bf16), V((2, 8, 2, 128, 256), bf16), V((16, 256, 256), bf16),
            V((2, 128, 256), f32), V((128, 256), f32), V((16, 2, 128, 128), bf16),
            V(sq, bf16), V(sq, bf16), V((32, 16, 128), bf16), V((32, 16, 128), bf16),
            V((32, 16, 128), bf16), V((32, 16, 128), bf16), V((3, 128, 128), bf16), V((3, 128, 128), bf16),
            V((256, 256), bf16), V((16, 256, 256), bf16), V((8, 256, 256), bf16),
            V((7, 256, 256), bf16), V((2, 8, 2, 128, 256), bf16), V((2, 4, 2, 128, 256), bf16),
            V((2, 2, 2, 128, 256), bf16), V((2, 2, 2, 128, 256), bf16), V((2, 2, 128, 256), bf16),
            dma((2, 8, 2)), dma, dma((2, 8, SUBS)), dma, dma((2,)), dma((3, 8, 2)), dma((2,)),
            dma, dma((32,)), dma, dma, dma, dma((32,)), dma, dma,
            dma((2,)), dma((2, 8, R_SUBS)), dma, dma, dma((2, 4, 2)), dma((2, 2, 2)), dma((2, 2, 2)), dma((2, 2)),
            V((128, 256), bf16), V((128, 256), bf16), V((128, 256), bf16), V((2, 128), f32),
            V((2, 128), f32), V((1, 128), f32), dma((9,)),
        ],
        compiler_params=pltpu.CompilerParams(
            collective_id=1, has_side_effects=True, vmem_limit_bytes=63 * 1024 * 1024
        ),
        name="layer",
    )(act, w, q, x, og, ld, wr, gain)


def shards(
    activations, w_value, query_input, key_input, log_decay, write_rate, norm_gain, out_grad
):
    return layer(
        activations, w_value, query_input, key_input, out_grad, log_decay, write_rate,
        norm_gain.reshape(1, -1),
    )


def solution(mesh):
    split = P("row", "col")
    flipped = P("col", "row")
    return jax.shard_map(
        shards,
        mesh=mesh,
        in_specs=(split, split, split, split, flipped, flipped, P(), split),
        out_specs=(split,) * 5,
        check_vma=False,
    )
```

```python
import functools

import jax
import jax.numpy as jnp
from jax import lax
from jax.experimental import pallas as pl
from jax.experimental.pallas import tpu as pltpu
from jax.sharding import PartitionSpec as P

MESH = pl.DeviceIdType.MESH
f32 = jnp.float32
bf16 = jnp.bfloat16
NN = (((1,), (0,)), ((), ()))
NT = (((1,), (1,)), ((), ()))
TN = (((0,), (0,)), ((), ()))


def dot(a, b, dims):
    return lax.dot_general(a, b, dims, preferred_element_type=f32)


def halves(a):
    high = a.astype(bf16)
    return high, (a - high.astype(f32)).astype(bf16)


def dot_left(a, b, dims):
    high, low = halves(a)
    return dot(high, b, dims) + dot(low, b, dims)


def dot_both(a, b, dims):
    a_high, a_low = halves(a)
    b_high, b_low = halves(b)
    return dot(a_high, b_high, dims) + (dot(a_high, b_low, dims) + dot(a_low, b_high, dims))


def key_terms(h, q, x, ld, wr, st):
    n = x.shape[0]
    rows = lax.broadcasted_iota(jnp.int32, (n, n), 0)
    cols = lax.broadcasted_iota(jnp.int32, (n, n), 1)
    lower = rows >= cols
    strict = rows > cols
    eye = rows == cols

    def col_of(row):
        return jnp.sum(jnp.where(eye, row, 0.0), axis=1, keepdims=True)

    def row_of(col):
        return jnp.sum(jnp.where(eye, col, 0.0), axis=0, keepdims=True)

    xf = x.astype(f32)
    rs = lax.rsqrt(jnp.sum(xf * xf, axis=1, keepdims=True) + 1e-06)
    rs_row = row_of(rs)
    g = jnp.sum(jnp.where(lower, ld, 0.0), axis=1, keepdims=True)
    g_row = row_of(g)
    total = jnp.sum(ld, axis=1, keepdims=True)
    decay = jnp.exp(g)
    decay_row = jnp.exp(g_row)
    tail = jnp.exp(total - g)
    b = col_of(wr)
    within = jnp.where(lower, jnp.exp(jnp.where(lower, g - g_row, 0.0)), 0.0)
    gram = dot(x, x, NT) * (rs * rs_row)
    coupling = jnp.where(strict, b * within * gram, 0.0)
    ident = jnp.where(eye, 1.0, 0.0)
    near = jnp.where((rows // 16) == (cols // 16), coupling, 0.0)
    inv = ident - near
    power = near
    yield
    for _ in range(3):
        power = dot_both(power, power, NN)
        inv = inv + dot_both(inv, power, NN)
        yield
    size = 16
    while size < n:
        off = ((rows // (2 * size)) == (cols // (2 * size))) & ((rows // size) != (cols // size))
        part = jnp.where(off, coupling, 0.0)
        inv = inv - dot_both(dot_both(inv, part, NN), inv, NN)
        size *= 2
        yield
    st["inv"][h] = inv
    st["within"][h] = within
    carry = dot_left(inv * (wr * decay_row * rs_row), x, NN)
    read = dot(q, x, NT) * within * rs_row
    loss = dot_left(carry * (tail * rs), x, TN) + jnp.where(eye, 1.0 - jnp.exp(total), 0.0)
    st["carry"][h] = carry
    st["read"][h] = read
    lanes = jnp.zeros((n, 128), f32)
    lane = lax.broadcasted_iota(jnp.int32, (n, 128), 1)
    for i, c in enumerate((rs, decay, tail, b)):
        lanes = jnp.where(lane == i, c, lanes)
    st["cols"][h] = lanes
    st["loss"][h] = loss.astype(bf16)


SUBS = 4
UNROLL = 4
FIRST = 3
ORDER = (
    "t", "w0", "a0123", "t", "w1", "a4567", "t", "t", "t", "s", "w2", "c01", "b01", "p",
    "w3", "b234", "c234", "l0", "w4", "b567", "c567", "l1", "w5", "d0123", "l2",
    "w6", "d4567", "l3", "w7", "x",
)
SUB = 256 // SUBS
R_SUBS = 4
R_SUB = 256 // R_SUBS


def layer_kernel(
    act_hbm, w_hbm, q_hbm, x_hbm, og_hbm, ld_hbm, wr_hbm, gain_hbm,
    out_ref, din_ref, dq_ref, dk_ref, dw_ref,
    inv, within, carry, read, cols, loss, fresh, grad_raw, summed, v_ref,
    act_own, act_all, w_all, part, part_in, loss_all,
    add, add2, got, got2, sent, sent2, state, grad,
    dv_all, w_terms, w_right, w_left, in_terms, in_sib, in_near, in_far, in_last,
    act_sem, act_sent, w_sem, w_sent, part_sem, loss_sem, loss_sent,
    s_send, s_recv, b_send, b_recv, t_send, t_recv, u_send, u_recv,
    dv_sem, r_sem, r_sent, i_sent, sib_sem, near_sem, far_sem, last_sem,
    q_ref, x_ref, og_ref, ld_ref, wr_ref, gain_ref, load_sem, loss_turned,
):
    n_row, n_z = 32, 16
    me, col = lax.axis_index("row"), lax.axis_index("col")
    a, z = me // n_z, me % n_z
    other = (1 - a) * n_z + z
    y, x_hi, core = col // 4, (col // 2) % 2, col % 2
    twin = col + 1 - 2 * core
    y_near = y + 1 - 2 * (y % 2)
    col_near = y_near * 4 + x_hi * 2 + core
    col_far = (3 - y) * 4 + x_hi * 2 + core
    source = a == y // 2
    first = jnp.where(source, y % 2, 1 - y % 2)
    slot = z // 2
    worker = z % 2 == 0
    up, down = a * n_z + (z + 1) % n_z, a * n_z + (z + n_z - 1) % n_z

    barrier = pltpu.get_barrier_semaphore()

    col_side = y * 4 + (1 - x_hi) * 2 + core
    for row_to, col_to in (
        (up, col), (down, col), (other, col), (me, twin), (me, col_near), (me, col_far),
        (me, col_side), (other, col_side),
    ):
        pl.semaphore_signal(barrier, inc=1, device_id=(row_to, col_to), device_id_type=MESH)
    w_own = w_all.at[z]
    loads = [
        pltpu.make_async_copy(act_hbm.at[:, pl.ds(i * 256, 256)], act_own.at[i], load_sem.at[i])
        for i in range(2)
    ] + [pltpu.make_async_copy(w_hbm, w_own, load_sem.at[2])]
    more = [
        pltpu.make_async_copy(src, dst, load_sem.at[3 + i])
        for i, (src, dst) in enumerate((
            (q_hbm, q_ref), (x_hbm, x_ref), (og_hbm, og_ref), (ld_hbm, ld_ref), (wr_hbm, wr_ref),
            (gain_hbm, gain_ref),
        ))
    ]
    for load in more + loads:
        load.start()

    st = dict(inv=inv, within=within, carry=carry, read=read, cols=cols, loss=loss)
    for load in more:
        load.wait()
    local = []
    for h in range(2):
        p = slice(h * 128, (h + 1) * 128)
        local.append(
            key_terms(h, q_ref[:, p], x_ref[:, p], ld_ref[h : h + 1, :], wr_ref[h : h + 1, :], st)
        )

    def think():
        for terms in local:
            next(terms, None)

    for _ in range(FIRST):
        think()
    for load in loads:
        load.wait()
    pl.semaphore_wait(barrier, 8)

    def remote(src, dst, send_sem, recv_sem, row_to, col_to):
        pltpu.make_async_remote_copy(
            src_ref=src, dst_ref=dst, send_sem=send_sem, recv_sem=recv_sem,
            device_id=(row_to, col_to), device_id_type=MESH,
        ).start()

    def landed(ref, sem):
        pltpu.make_async_copy(ref, ref, sem).wait()

    home_row = (y // 2) * n_z + z
    for xh in range(2):
        to_col = y * 4 + xh * 2 + core
        here = source & (x_hi == xh)
        for f in range(2):
            dst, sem = act_all.at[a, col % 8, f], act_sem.at[a, col % 8, f]

            @pl.when(jnp.logical_not(here))
            def _():
                remote(act_own.at[f], dst, act_sent, sem, home_row, to_col)

            @pl.when(here)
            def _():
                pltpu.make_async_copy(act_own.at[f], dst, sem).start()

    def act_first(i, is_source):
        t, xh, f = i // 4, (i // 2) % 2, i % 2
        cc = first * 4 + xh * 2 + core
        ref, sem = act_all.at[t, cc, f], act_sem.at[t, cc, f]
        landed(ref, sem)

        if is_source:
            remote(ref, ref, act_sent, sem, me, col_far)
        remote(ref, ref, act_sent, sem, me, col_near)
        remote(ref, ref, act_sent, sem, me, twin)

    def act_second(i):
        t, xh, f = i // 4, (i // 2) % 2, i % 2
        cc = (1 - first) * 4 + xh * 2 + core
        ref, sem = act_all.at[t, cc, f], act_sem.at[t, cc, f]
        landed(ref, sem)
        remote(ref, ref, act_sent, sem, me, twin)

    def act_last():
        for t in range(2):
            for k in range(4):
                cc = k * 2 + (1 - core)
                for f in range(2):
                    landed(act_all.at[t, cc, f], act_sem.at[t, cc, f])

    def w_piece(s, way, sub, origin):
        ref = w_all.at[origin, pl.ds(sub * SUB, SUB), :]
        return ref, w_sem.at[way, s, sub]

    def w_send(s, way):
        origin = (z + n_z - s) % n_z if way == 0 else (z + s) % n_z
        for sub in range(SUBS):
            ref, sem = w_piece(s, way, sub, origin)
            remote(ref, ref, w_sent, sem, up if way == 0 else down, col)

    def w_step(s):
        for sub in range(SUBS):
            for way in range(2):
                if way == 1 and s == 7:
                    continue
                origin = (z + n_z - s - 1) % n_z if way == 0 else (z + s + 1) % n_z
                ref, sem = w_piece(s, way, sub, origin)
                landed(ref, sem)
                if s + 1 < (8 if way == 0 else 7):
                    _, after = w_piece(s + 1, way, sub, origin)
                    remote(ref, ref, w_sent, after, up if way == 0 else down, col)

    w_send(0, 0)
    w_send(0, 1)

    def loss_send(k, s):
        for way in range(2):
            if s >= (8 if way == 0 else 7):
                continue
            origin = (z + n_z - s) % n_z if way == 0 else (z + s) % n_z
            owner = a if k == 0 else 1 - a
            ref = loss_all.at[origin, owner]
            remote(ref, ref, loss_sent.at[1], loss_sem.at[way, s, owner], up if way == 0 else down, col)

    def loss_start():
        remote(loss.at[1 - a], loss_all.at[z, a], loss_sent.at[0], loss_sem.at[2, 0, 0], other, col)
        loss_all[z, a] = loss[a]
        loss_send(0, 0)

    def loss_first():
        landed(loss_all.at[z, 1 - a], loss_sem.at[2, 0, 0])
        loss_send(1, 0)

    def loss_step(s):
        for k in range(2):
            owner = a if k == 0 else 1 - a
            for way in range(2):
                if way == 1 and s == 7:
                    continue
                origin = (z + n_z - s - 1) % n_z if way == 0 else (z + s + 1) % n_z
                landed(loss_all.at[origin, owner], loss_sem.at[way, s, owner])
            loss_send(k, s + 1)

    def at_source(work):
        pl.when(source)(work)

    def at_sink(work):
        pl.when(jnp.logical_not(source))(work)

    def each(work, numbers, *rest):
        for number in numbers:
            work(int(number), *rest)

    for item in ORDER:
        what, number = item[0], item[1:]
        if what == "t":
            think()
        elif what == "w":
            w_step(int(number))
        elif what == "a":
            at_source(functools.partial(each, act_first, number, True))
        elif what == "b":
            at_sink(functools.partial(each, act_first, number, False))
        elif what == "c":
            at_source(functools.partial(each, act_second, number))
        elif what == "d":
            at_sink(functools.partial(each, act_second, number))
        elif what == "s":
            loss_start()
        elif what == "p":
            loss_first()
        elif what == "l":
            loss_step(int(number))
        elif what == "x":
            act_last()

    total = jnp.zeros((256, 256), f32)
    for k in range(n_z):
        both = jnp.concatenate([act_all[0, k // 2, k % 2], act_all[1, k // 2, k % 2]], axis=0)
        total = total + dot(both, w_all[k], NN)
    part[0] = total[:128]
    part[1] = total[128:]
    remote(part.at[1 - a], part_in, part_sem.at[0], part_sem.at[1], other, col)
    loss_step(4)
    landed(part_in, part_sem.at[1])
    v_ref[...] = (part[a] + part_in[...]).astype(bf16)
    loss_step(5)

    lane_rows = pl.ds(pl.multiple_of(slot * 16, 16), 16)

    def deal(src, dst, send_sem, recv_sem):
        for j in (4, 12, 5, 13, 3, 11, 6, 14, 2, 10, 7, 15, 1, 9, 8, 0):
            k = (1 - a + j // 8) % 2 * 8 + (slot + j) % 8
            block = src.at[k // 8, pl.ds(pl.multiple_of((k % 8) * 16, 16), 16), :]
            to = (k // 8) * n_z + (k % 8) * 2
            if j != 8:
                remote(block, dst.at[me], send_sem, recv_sem.at[me], to, col)
            else:
                @pl.when(worker)
                def _():
                    pltpu.make_async_copy(block, dst.at[me], recv_sem.at[me]).start()

                @pl.when(jnp.logical_not(worker))
                def _():
                    remote(block, dst.at[me], send_sem, recv_sem.at[me], to, col)

    def give_back(i, src, dst, send_sem, recv_sem):
        mine = i == me
        remote(
            src.at[i], dst.at[jnp.where(mine, 2, a), lane_rows, :], send_sem, recv_sem,
            jnp.where(mine, other, i), col,
        )

    for h in range(2):
        p = slice(h * 128, (h + 1) * 128)
        c = cols[h]
        rs, tail = c[:, 0:1], c[:, 2:3]
        u = dot_left(inv[h] * wr_ref[h : h + 1, :], v_ref[:, p], NN)
        fresh[h] = u
        add[h] = dot_left(u * (tail * rs), x_ref[:, p], TN).astype(bf16)

    deal(add, got, s_send, s_recv)
    loss_step(6)
    loss_step(7)

    @pl.when(worker)
    def _():
        def step(i, s):
            s_low = s.astype(bf16)
            sent[i] = s_low
            give_back(i, sent, state, b_send, b_recv)
            landed(got.at[i], s_recv.at[i])
            return s - dot(s_low, loss_all[i % 16, i // 16], NN) + got[i].astype(f32)

        lax.fori_loop(0, n_row, step, jnp.zeros((16, 128), f32), unroll=UNROLL)
        state[a, lane_rows, :] = sent[me]

        def turn(i, _):
            loss_turned[i] = loss_all[i % 16, i // 16].T
            return 0

        lax.fori_loop(0, n_row, turn, 0, unroll=UNROLL)

    landed(state.at[pl.ds(0, 2)], b_recv)

    gain = gain_ref[0:1, :]
    for h in range(2):
        p = slice(h * 128, (h + 1) * 128)
        c = cols[h]
        decay = c[:, 1:2]
        s = state[h]
        u = fresh[h] - dot_left(carry[h], s, NT)
        fresh[h] = u
        raw = decay * dot(q_ref[:, p], s, NT) + dot_both(read[h], u, NN)
        r = lax.rsqrt(jnp.mean(raw * raw, axis=1, keepdims=True) + 1e-06)
        out_ref[:, p] = (raw * r * gain).astype(bf16)
        gg = og_ref[:, p].astype(f32) * gain
        d_raw = r * gg - raw * (r * r * r * jnp.mean(raw * gg, axis=1, keepdims=True))
        grad_raw[h] = d_raw
        back = dot_both(read[h], d_raw, TN)
        summed[h] = back
        add2[h] = (dot_left(decay * d_raw, q_ref[:, p], TN) - dot_both(back, carry[h], TN)).astype(bf16)

    deal(add2, got2, t_send, t_recv)

    @pl.when(worker)
    def _():
        def step(k, s):
            i = n_row - 1 - k
            s_low = s.astype(bf16)
            sent2[i] = s_low
            give_back(i, sent2, grad, u_send, u_recv)
            landed(got2.at[i], t_recv.at[i])
            return s - dot(s_low, loss_turned[i], NN) + got2[i].astype(f32)

        lax.fori_loop(0, n_row, step, jnp.zeros((16, 128), f32), unroll=UNROLL)
        grad[a, lane_rows, :] = sent2[me]

    landed(grad.at[pl.ds(0, 2)], u_recv)

    n = 128
    rows_i = lax.broadcasted_iota(jnp.int32, (n, n), 0)
    cols_i = lax.broadcasted_iota(jnp.int32, (n, n), 1)
    own_tokens = pl.ds(pl.multiple_of(a * 128, 128), 128)
    later = []
    for h in range(2):
        p = slice(h * 128, (h + 1) * 128)
        c = cols[h]
        rs, tail, b = c[:, 0:1], c[:, 2:3], c[:, 3:4]
        d_u = summed[h] + (tail * rs) * dot(x_ref[:, p], grad[h], NT)
        grown = dot_both(inv[h], d_u, TN)
        later.append(grown)
        dv_all[own_tokens, p] = (b * grown).astype(bf16)
    mine = dv_all.at[own_tokens, :]
    remote(mine, mine, dv_sem.at[0], dv_sem.at[1], other, col)

    def query_key_grads(h):
        p = slice(h * 128, (h + 1) * 128)
        q, x = q_ref[:, p], x_ref[:, p]
        c = cols[h]
        rs, decay, tail, b = c[:, 0:1], c[:, 1:2], c[:, 2:3], c[:, 3:4]
        s, g, u, d_raw, grown = state[h], grad[h], fresh[h], grad_raw[h], later[h]
        rs_row = jnp.sum(jnp.where(rows_i == cols_i, rs, 0.0), axis=0, keepdims=True)
        d_read = dot_both(d_raw, u, NT) * within[h]
        dq_ref[:, p] = (decay * dot_left(d_raw, s, NN) + dot_left(d_read * rs_row, x, NN)).astype(bf16)
        d_gram = jnp.where(rows_i > cols_i, -b * within[h] * dot_both(grown, u, NT), 0.0)
        d_k = (
            dot_left(d_read, q, TN)
            + tail * dot_left(u, g, NN)
            - (b * decay) * dot_left(grown, s, NN)
            + dot_left(d_gram * rs_row, x, NN)
            + dot_left(d_gram * rs, x, TN)
        )
        unit = rs * x.astype(f32)
        dk_ref[:, p] = (rs * (d_k - unit * jnp.sum(unit * d_k, axis=1, keepdims=True))).astype(bf16)

    theirs = dv_all.at[pl.ds(pl.multiple_of((1 - a) * 128, 128), 128), :]
    landed(theirs, dv_sem.at[1])

    def w_term(d):
        acc = dot(act_all[0, d // 2, d % 2], dv_all[0:128, :], TN)
        return acc + dot(act_all[1, d // 2, d % 2], dv_all[128:256, :], TN)

    def r_dest(s, way):
        return (z + 8 - s) % n_z if way == 0 else (z + n_z - 7 + s) % n_z

    def r_slot(s, way):
        return w_right.at[s] if way == 0 else w_left.at[s]

    def r_send(s, way):
        d = r_dest(s, way)
        for sub in range(R_SUBS):
            q = pl.ds(sub * R_SUB, R_SUB)
            if s > 0:
                landed(r_slot(s - 1, way).at[q, :], r_sem.at[way, s - 1, sub])
                w_terms[d, q, :] = (
                    w_terms[d, q, :].astype(f32) + r_slot(s - 1, way)[q, :].astype(f32)
                ).astype(bf16)
            remote(w_terms.at[d, q, :], r_slot(s, way).at[q, :], r_sent, r_sem.at[way, s, sub],
                   up if way == 0 else down, col)

    def r_make(s):
        for way in range(2):
            if way == 1 and s == 7:
                continue
            d = r_dest(s, way)
            w_terms[d] = w_term(d).astype(bf16)

    def r_step(s):
        for way in range(2):
            if way == 1 and s == 7:
                continue
            r_send(s, way)

    def in_make(cc):
        for i in range(2):
            both = dot(dv_all[...], w_all[cc * 2 + i], NT).astype(bf16)
            for t in range(2):
                in_terms[t, cc, i] = both[t * 128 : (t + 1) * 128]

    def plus(t, cc, f, ref):
        in_terms[t, cc, f] = (in_terms[t, cc, f].astype(f32) + ref[...].astype(f32)).astype(bf16)

    def sib_send(k):
        cc = k * 2 + 1 - core
        in_make(cc)
        for t in range(2):
            for f in range(2):
                remote(in_terms.at[t, cc, f], in_sib.at[t, k, f], i_sent, sib_sem.at[t, k, f], me, twin)

    def own_make(k):
        in_make(k * 2 + core)

    def near_send(i):
        t, xh, f = i // 4, (i // 2) % 2, i % 2
        k = (1 - first) * 2 + xh
        cc = k * 2 + core
        landed(in_sib.at[t, k, f], sib_sem.at[t, k, f])
        plus(t, cc, f, in_sib.at[t, k, f])
        remote(in_terms.at[t, cc, f], in_near.at[t, xh, f], i_sent, near_sem.at[t, xh, f], me, col_near)

    def far_send(i):
        t, xh, f = i // 4, (i // 2) % 2, i % 2
        k = first * 2 + xh
        cc = k * 2 + core
        landed(in_sib.at[t, k, f], sib_sem.at[t, k, f])
        plus(t, cc, f, in_sib.at[t, k, f])
        landed(in_near.at[t, xh, f], near_sem.at[t, xh, f])
        plus(t, cc, f, in_near.at[t, xh, f])

        @pl.when(jnp.logical_not(source))
        def _():
            remote(in_terms.at[t, cc, f], in_far.at[t, xh, f], i_sent, far_sem.at[t, xh, f], me, col_far)

    def home_send(i):
        t, xh, f = i // 4, (i // 2) % 2, i % 2
        k = first * 2 + xh
        cc = k * 2 + core

        @pl.when(source)
        def _():
            landed(in_far.at[t, xh, f], far_sem.at[t, xh, f])
            plus(t, cc, f, in_far.at[t, xh, f])
            row_to, col_to = t * n_z + z, y * 4 + xh * 2 + core
            here = (row_to == me) & (col_to == col)
            dst, sem = in_last.at[x_hi, f], last_sem.at[x_hi, f]

            @pl.when(jnp.logical_not(here))
            def _():
                remote(in_terms.at[t, cc, f], dst, i_sent, sem, row_to, col_to)

            @pl.when(here)
            def _():
                pltpu.make_async_copy(in_terms.at[t, cc, f], dst, sem).start()

    r_make(0)
    r_step(0)
    for k in range(4):
        sib_send(k)
    r_make(1)
    for k in range(4):
        own_make(k)
    r_step(1)
    r_make(2)
    for i in range(4):
        near_send(i)
    r_step(2)
    for i in range(4, 8):
        near_send(i)
    r_make(3)
    query_key_grads(0)
    r_step(3)
    r_make(4)
    for i in range(4):
        far_send(i)
    r_step(4)
    r_make(5)
    for i in range(4, 8):
        far_send(i)
    query_key_grads(1)
    r_step(5)
    r_make(6)
    for i in range(4):
        home_send(i)
    r_step(6)
    r_make(7)
    for i in range(4, 8):
        home_send(i)
    r_step(7)
    own_term = w_term(z)
    for xh in range(2):
        for f in range(2):
            landed(in_last.at[xh, f], last_sem.at[xh, f])
    for i in range(2):
        din_ref[:, i * 256 : (i + 1) * 256] = (
            in_last[0, i].astype(f32) + in_last[1, i].astype(f32)
        ).astype(bf16)
    for sub in range(R_SUBS):
        q = pl.ds(sub * R_SUB, R_SUB)
        landed(w_right.at[7, q, :], r_sem.at[0, 7, sub])
        landed(w_left.at[6, q, :], r_sem.at[1, 6, sub])
    dw_ref[...] = own_term + w_right[7].astype(f32) + w_left[6].astype(f32)

    def drain(ref, count, sem):
        def one(i, _):
            pltpu.make_async_copy(ref, ref, sem).wait()
            return 0
        lax.fori_loop(0, count, one, 0)

    big = act_own.at[0]
    own = jnp.where(worker, 1, 0)
    far = jnp.where(source, 1, 0)
    self_home = jnp.where(source, 1, 0)
    drain(big, (2 - self_home + 4 + 4 * far + 8) * 2, act_sent)
    drain(w_all.at[0, pl.ds(0, SUB), :], 15 * SUBS, w_sent)
    landed(part.at[0], part_sem.at[0])
    landed(loss.at[0], loss_sent.at[0])
    drain(loss.at[0], 30, loss_sent.at[1])
    drain(got.at[0], 16 - own, s_send)
    drain(got.at[0], 16 - own, t_send)

    @pl.when(worker)
    def _():
        drain(got.at[0], n_row, b_send)
        drain(got.at[0], n_row, u_send)

    landed(mine, dv_sem.at[0])
    drain(w_all.at[0, pl.ds(0, R_SUB), :], 15 * R_SUBS, r_sent)
    drain(big, (8 + 4 + 4 * (1 - far) + (4 - 1) * far) * 2, i_sent)


def layer(act, w, q, x, og, ld, wr, gain):
    sq = (2, 128, 128)
    vm = pl.BlockSpec(memory_space=pltpu.VMEM)
    o = jax.ShapeDtypeStruct((128, 256), bf16)
    dma = pltpu.SemaphoreType.DMA
    V = pltpu.VMEM
    return pl.pallas_call(
        layer_kernel,
        out_shape=(
            o,
            jax.ShapeDtypeStruct((128, 512), bf16),
            o,
            o,
            jax.ShapeDtypeStruct((256, 256), f32),
        ),
        in_specs=[pl.BlockSpec(memory_space=pltpu.HBM)] * 8,
        out_specs=(vm,) * 5,
        scratch_shapes=[
            V(sq, f32), V(sq, f32), V(sq, f32), V(sq, f32), V(sq, f32), V(sq, bf16),
            V(sq, f32), V(sq, f32), V(sq, f32), V((128, 256), bf16),
            V((2, 128, 256), bf16), V((2, 8, 2, 128, 256), bf16), V((16, 256, 256), bf16),
            V((2, 128, 256), f32), V((128, 256), f32), V((16, 2, 128, 128), bf16),
            V(sq, bf16), V(sq, bf16), V((32, 16, 128), bf16), V((32, 16, 128), bf16),
            V((32, 16, 128), bf16), V((32, 16, 128), bf16), V((3, 128, 128), bf16), V((3, 128, 128), bf16),
            V((256, 256), bf16), V((16, 256, 256), bf16), V((8, 256, 256), bf16),
            V((7, 256, 256), bf16), V((2, 8, 2, 128, 256), bf16), V((2, 4, 2, 128, 256), bf16),
            V((2, 2, 2, 128, 256), bf16), V((2, 2, 2, 128, 256), bf16), V((2, 2, 128, 256), bf16),
            dma((2, 8, 2)), dma, dma((2, 8, SUBS)), dma, dma((2,)), dma((3, 8, 2)), dma((2,)),
            dma, dma((32,)), dma, dma, dma, dma((32,)), dma, dma,
            dma((2,)), dma((2, 8, R_SUBS)), dma, dma, dma((2, 4, 2)), dma((2, 2, 2)), dma((2, 2, 2)), dma((2, 2)),
            V((128, 256), bf16), V((128, 256), bf16), V((128, 256), bf16), V((2, 128), f32),
            V((2, 128), f32), V((1, 128), f32), dma((9,)), V((32, 128, 128), bf16),
        ],
        compiler_params=pltpu.CompilerParams(
            collective_id=1, has_side_effects=True, vmem_limit_bytes=63 * 1024 * 1024
        ),
        name="layer",
    )(act, w, q, x, og, ld, wr, gain)


def finish_kernel(*refs):
    for src, dst in zip(refs[:5], refs[5:]):
        dst[...] = src[...]


def finished(results):
    return pl.pallas_call(
        finish_kernel,
        out_shape=tuple(jax.ShapeDtypeStruct(r.shape, r.dtype) for r in results),
        name="finish",
    )(*results)


def shards(
    activations, w_value, query_input, key_input, log_decay, write_rate, norm_gain, out_grad
):
    return finished(layer(
        activations, w_value, query_input, key_input, out_grad, log_decay, write_rate,
        norm_gain.reshape(1, -1),
    ))


def solution(mesh):
    split = P("row", "col")
    flipped = P("col", "row")
    return jax.shard_map(
        shards,
        mesh=mesh,
        in_specs=(split, split, split, split, flipped, flipped, P(), split),
        out_specs=(split,) * 5,
        check_vma=False,
    )
```

```python
import functools

import jax
import jax.numpy as jnp
from jax import lax
from jax.experimental import pallas as pl
from jax.experimental.pallas import tpu as pltpu
from jax.sharding import PartitionSpec as P

MESH = pl.DeviceIdType.MESH
f32 = jnp.float32
bf16 = jnp.bfloat16
NN = (((1,), (0,)), ((), ()))
NT = (((1,), (1,)), ((), ()))
TN = (((0,), (0,)), ((), ()))


def dot(a, b, dims):
    return lax.dot_general(a, b, dims, preferred_element_type=f32)


def halves(a):
    high = a.astype(bf16)
    return high, (a - high.astype(f32)).astype(bf16)


def dot_left(a, b, dims):
    high, low = halves(a)
    return dot(high, b, dims) + dot(low, b, dims)


def dot_both(a, b, dims):
    a_high, a_low = halves(a)
    b_high, b_low = halves(b)
    return dot(a_high, b_high, dims) + (dot(a_high, b_low, dims) + dot(a_low, b_high, dims))


def key_terms(h, q, x, ld, wr, st):
    n = x.shape[0]
    rows = lax.broadcasted_iota(jnp.int32, (n, n), 0)
    cols = lax.broadcasted_iota(jnp.int32, (n, n), 1)
    lower = rows >= cols
    strict = rows > cols
    eye = rows == cols

    def col_of(row):
        return jnp.sum(jnp.where(eye, row, 0.0), axis=1, keepdims=True)

    def row_of(col):
        return jnp.sum(jnp.where(eye, col, 0.0), axis=0, keepdims=True)

    xf = x.astype(f32)
    rs = lax.rsqrt(jnp.sum(xf * xf, axis=1, keepdims=True) + 1e-06)
    rs_row = row_of(rs)
    g = jnp.sum(jnp.where(lower, ld, 0.0), axis=1, keepdims=True)
    g_row = row_of(g)
    total = jnp.sum(ld, axis=1, keepdims=True)
    decay = jnp.exp(g)
    decay_row = jnp.exp(g_row)
    tail = jnp.exp(total - g)
    b = col_of(wr)
    within = jnp.where(lower, jnp.exp(jnp.where(lower, g - g_row, 0.0)), 0.0)
    gram = dot(x, x, NT) * (rs * rs_row)
    coupling = jnp.where(strict, b * within * gram, 0.0)
    ident = jnp.where(eye, 1.0, 0.0)
    near = jnp.where((rows // 16) == (cols // 16), coupling, 0.0)
    inv = ident - near
    power = near
    yield
    for _ in range(3):
        power = dot_both(power, power, NN)
        inv = inv + dot_both(inv, power, NN)
        yield
    size = 16
    while size < n:
        off = ((rows // (2 * size)) == (cols // (2 * size))) & ((rows // size) != (cols // size))
        part = jnp.where(off, coupling, 0.0)
        inv = inv - dot_both(dot_both(inv, part, NN), inv, NN)
        size *= 2
        yield
    st["inv"][h] = inv
    st["within"][h] = within
    carry = dot_left(inv * (wr * decay_row * rs_row), x, NN)
    read = dot(q, x, NT) * within * rs_row
    loss = dot_left(carry * (tail * rs), x, TN) + jnp.where(eye, 1.0 - jnp.exp(total), 0.0)
    st["carry"][h] = carry
    st["read"][h] = read
    lanes = jnp.zeros((n, 128), f32)
    lane = lax.broadcasted_iota(jnp.int32, (n, 128), 1)
    for i, c in enumerate((rs, decay, tail, b)):
        lanes = jnp.where(lane == i, c, lanes)
    st["cols"][h] = lanes
    st["loss"][h] = loss.astype(bf16)


SUBS = 4
UNROLL = 4
FIRST = 3
ORDER = (
    "t", "w0", "a0123", "t", "w1", "a4567", "t", "t", "t", "s", "w2", "c01", "b01", "p",
    "w3", "b234", "c234", "l0", "w4", "b567", "c567", "l1", "w5", "d0123", "l2",
    "w6", "d4567", "l3", "w7", "x",
)
SUB = 256 // SUBS
R_SUBS = 4
R_SUB = 256 // R_SUBS


def layer_kernel(
    act_hbm, w_hbm, q_hbm, x_hbm, og_hbm, ld_hbm, wr_hbm, gain_hbm,
    out_ref, din_ref, dq_ref, dk_ref, dw_ref,
    inv, within, carry, read, cols, loss, fresh, grad_raw, summed, v_ref,
    act_own, act_all, w_all, part, part_in, loss_all,
    add, add2, got, got2, sent, sent2, state, grad,
    dv_all, w_terms, w_right, w_left, in_terms, in_sib, in_near, in_far, in_last,
    act_sem, act_sent, w_sem, w_sent, part_sem, loss_sem, loss_sent,
    s_send, s_recv, b_send, b_recv, t_send, t_recv, u_send, u_recv,
    dv_sem, r_sem, r_sent, i_sent, sib_sem, near_sem, far_sem, last_sem,
    q_ref, x_ref, og_ref, ld_ref, wr_ref, gain_ref, load_sem, loss_turned,
):
    n_row, n_z = 32, 16
    me, col = lax.axis_index("row"), lax.axis_index("col")
    a, z = me // n_z, me % n_z
    other = (1 - a) * n_z + z
    y, x_hi, core = col // 4, (col // 2) % 2, col % 2
    twin = col + 1 - 2 * core
    y_near = y + 1 - 2 * (y % 2)
    col_near = y_near * 4 + x_hi * 2 + core
    col_far = (3 - y) * 4 + x_hi * 2 + core
    source = a == y // 2
    first = jnp.where(source, y % 2, 1 - y % 2)
    slot = z // 2
    worker = z % 2 == 0
    up, down = a * n_z + (z + 1) % n_z, a * n_z + (z + n_z - 1) % n_z

    barrier = pltpu.get_barrier_semaphore()

    col_side = y * 4 + (1 - x_hi) * 2 + core
    for row_to, col_to in (
        (up, col), (down, col), (other, col), (me, twin), (me, col_near), (me, col_far),
        (me, col_side), (other, col_side),
    ):
        pl.semaphore_signal(barrier, inc=1, device_id=(row_to, col_to), device_id_type=MESH)
    w_own = w_all.at[z]
    loads = [
        pltpu.make_async_copy(act_hbm.at[:, pl.ds(i * 256, 256)], act_own.at[i], load_sem.at[i])
        for i in range(2)
    ] + [pltpu.make_async_copy(w_hbm, w_own, load_sem.at[2])]
    more = [
        pltpu.make_async_copy(src, dst, load_sem.at[3 + i])
        for i, (src, dst) in enumerate((
            (q_hbm, q_ref), (x_hbm, x_ref), (og_hbm, og_ref), (ld_hbm, ld_ref), (wr_hbm, wr_ref),
            (gain_hbm, gain_ref),
        ))
    ]
    for load in more + loads:
        load.start()

    st = dict(inv=inv, within=within, carry=carry, read=read, cols=cols, loss=loss)
    for load in more:
        load.wait()
    local = []
    for h in range(2):
        p = slice(h * 128, (h + 1) * 128)
        local.append(
            key_terms(h, q_ref[:, p], x_ref[:, p], ld_ref[h : h + 1, :], wr_ref[h : h + 1, :], st)
        )

    def think():
        for terms in local:
            next(terms, None)

    for _ in range(FIRST):
        think()
    for load in loads:
        load.wait()
    pl.semaphore_wait(barrier, 8)

    def remote(src, dst, send_sem, recv_sem, row_to, col_to):
        pltpu.make_async_remote_copy(
            src_ref=src, dst_ref=dst, send_sem=send_sem, recv_sem=recv_sem,
            device_id=(row_to, col_to), device_id_type=MESH,
        ).start()

    def landed(ref, sem):
        pltpu.make_async_copy(ref, ref, sem).wait()

    home_row = (y // 2) * n_z + z
    for xh in range(2):
        to_col = y * 4 + xh * 2 + core
        here = source & (x_hi == xh)
        for f in range(2):
            dst, sem = act_all.at[a, col % 8, f], act_sem.at[a, col % 8, f]

            @pl.when(jnp.logical_not(here))
            def _():
                remote(act_own.at[f], dst, act_sent, sem, home_row, to_col)

            @pl.when(here)
            def _():
                pltpu.make_async_copy(act_own.at[f], dst, sem).start()

    def act_first(i, is_source):
        t, xh, f = i // 4, (i // 2) % 2, i % 2
        cc = first * 4 + xh * 2 + core
        ref, sem = act_all.at[t, cc, f], act_sem.at[t, cc, f]
        landed(ref, sem)

        if is_source:
            remote(ref, ref, act_sent, sem, me, col_far)
        remote(ref, ref, act_sent, sem, me, col_near)
        remote(ref, ref, act_sent, sem, me, twin)

    def act_second(i):
        t, xh, f = i // 4, (i // 2) % 2, i % 2
        cc = (1 - first) * 4 + xh * 2 + core
        ref, sem = act_all.at[t, cc, f], act_sem.at[t, cc, f]
        landed(ref, sem)
        remote(ref, ref, act_sent, sem, me, twin)

    def act_last():
        for t in range(2):
            for k in range(4):
                cc = k * 2 + (1 - core)
                for f in range(2):
                    landed(act_all.at[t, cc, f], act_sem.at[t, cc, f])

    def w_piece(s, way, sub, origin):
        ref = w_all.at[origin, pl.ds(sub * SUB, SUB), :]
        return ref, w_sem.at[way, s, sub]

    def w_send(s, way):
        origin = (z + n_z - s) % n_z if way == 0 else (z + s) % n_z
        for sub in range(SUBS):
            ref, sem = w_piece(s, way, sub, origin)
            remote(ref, ref, w_sent, sem, up if way == 0 else down, col)

    def w_step(s):
        for sub in range(SUBS):
            for way in range(2):
                if way == 1 and s == 7:
                    continue
                origin = (z + n_z - s - 1) % n_z if way == 0 else (z + s + 1) % n_z
                ref, sem = w_piece(s, way, sub, origin)
                landed(ref, sem)
                if s + 1 < (8 if way == 0 else 7):
                    _, after = w_piece(s + 1, way, sub, origin)
                    remote(ref, ref, w_sent, after, up if way == 0 else down, col)

    w_send(0, 0)
    w_send(0, 1)

    def loss_send(k, s):
        for way in range(2):
            if s >= (8 if way == 0 else 7):
                continue
            origin = (z + n_z - s) % n_z if way == 0 else (z + s) % n_z
            owner = a if k == 0 else 1 - a
            ref = loss_all.at[origin, owner]
            remote(ref, ref, loss_sent.at[1], loss_sem.at[way, s, owner], up if way == 0 else down, col)

    def loss_start():
        remote(loss.at[1 - a], loss_all.at[z, a], loss_sent.at[0], loss_sem.at[2, 0, 0], other, col)
        loss_all[z, a] = loss[a]
        loss_send(0, 0)

    def loss_first():
        landed(loss_all.at[z, 1 - a], loss_sem.at[2, 0, 0])
        loss_send(1, 0)

    def loss_step(s):
        for k in range(2):
            owner = a if k == 0 else 1 - a
            for way in range(2):
                if way == 1 and s == 7:
                    continue
                origin = (z + n_z - s - 1) % n_z if way == 0 else (z + s + 1) % n_z
                landed(loss_all.at[origin, owner], loss_sem.at[way, s, owner])
            loss_send(k, s + 1)

    def at_source(work):
        pl.when(source)(work)

    def at_sink(work):
        pl.when(jnp.logical_not(source))(work)

    def each(work, numbers, *rest):
        for number in numbers:
            work(int(number), *rest)

    for item in ORDER:
        what, number = item[0], item[1:]
        if what == "t":
            think()
        elif what == "w":
            w_step(int(number))
        elif what == "a":
            at_source(functools.partial(each, act_first, number, True))
        elif what == "b":
            at_sink(functools.partial(each, act_first, number, False))
        elif what == "c":
            at_source(functools.partial(each, act_second, number))
        elif what == "d":
            at_sink(functools.partial(each, act_second, number))
        elif what == "s":
            loss_start()
        elif what == "p":
            loss_first()
        elif what == "l":
            loss_step(int(number))
        elif what == "x":
            act_last()

    total = jnp.zeros((256, 256), f32)
    for k in range(n_z):
        both = jnp.concatenate([act_all[0, k // 2, k % 2], act_all[1, k // 2, k % 2]], axis=0)
        total = total + dot(both, w_all[k], NN)
    part[0] = total[:128]
    part[1] = total[128:]
    remote(part.at[1 - a], part_in, part_sem.at[0], part_sem.at[1], other, col)
    loss_step(4)
    landed(part_in, part_sem.at[1])
    v_ref[...] = (part[a] + part_in[...]).astype(bf16)
    loss_step(5)

    lane_rows = pl.ds(pl.multiple_of(slot * 16, 16), 16)

    def deal(src, dst, send_sem, recv_sem):
        for j in (4, 12, 5, 13, 3, 11, 6, 14, 2, 10, 7, 15, 1, 9, 8, 0):
            k = (1 - a + j // 8) % 2 * 8 + (slot + j) % 8
            block = src.at[k // 8, pl.ds(pl.multiple_of((k % 8) * 16, 16), 16), :]
            to = (k // 8) * n_z + (k % 8) * 2
            if j != 8:
                remote(block, dst.at[me], send_sem, recv_sem.at[me], to, col)
            else:
                @pl.when(worker)
                def _():
                    pltpu.make_async_copy(block, dst.at[me], recv_sem.at[me]).start()

                @pl.when(jnp.logical_not(worker))
                def _():
                    remote(block, dst.at[me], send_sem, recv_sem.at[me], to, col)

    def give_back(i, src, dst, send_sem, recv_sem):
        mine = i == me
        remote(
            src.at[i], dst.at[jnp.where(mine, 2, a), lane_rows, :], send_sem, recv_sem,
            jnp.where(mine, other, i), col,
        )

    for h in range(2):
        p = slice(h * 128, (h + 1) * 128)
        c = cols[h]
        rs, tail = c[:, 0:1], c[:, 2:3]
        u = dot_left(inv[h] * wr_ref[h : h + 1, :], v_ref[:, p], NN)
        fresh[h] = u
        add[h] = dot_left(u * (tail * rs), x_ref[:, p], TN).astype(bf16)

    deal(add, got, s_send, s_recv)
    loss_step(6)
    loss_step(7)

    @pl.when(worker)
    def _():
        def step(i, s):
            s_low = s.astype(bf16)
            kept = s - dot(s_low, loss_all[i % 16, i // 16], NN)
            sent[i] = s_low
            give_back(i, sent, state, b_send, b_recv)
            landed(got.at[i], s_recv.at[i])
            return kept + got[i].astype(f32)

        lax.fori_loop(0, n_row, step, jnp.zeros((16, 128), f32), unroll=UNROLL)
        state[a, lane_rows, :] = sent[me]

        def turn(i, _):
            loss_turned[i] = loss_all[i % 16, i // 16].T
            return 0

        lax.fori_loop(0, n_row, turn, 0, unroll=UNROLL)

    landed(state.at[pl.ds(0, 2)], b_recv)

    gain = gain_ref[0:1, :]
    for h in range(2):
        p = slice(h * 128, (h + 1) * 128)
        c = cols[h]
        decay = c[:, 1:2]
        s = state[h]
        u = fresh[h] - dot_left(carry[h], s, NT)
        fresh[h] = u
        raw = decay * dot(q_ref[:, p], s, NT) + dot_both(read[h], u, NN)
        r = lax.rsqrt(jnp.mean(raw * raw, axis=1, keepdims=True) + 1e-06)
        out_ref[:, p] = (raw * r * gain).astype(bf16)
        gg = og_ref[:, p].astype(f32) * gain
        d_raw = r * gg - raw * (r * r * r * jnp.mean(raw * gg, axis=1, keepdims=True))
        grad_raw[h] = d_raw
        back = dot_both(read[h], d_raw, TN)
        summed[h] = back
        add2[h] = (dot_left(decay * d_raw, q_ref[:, p], TN) - dot_both(back, carry[h], TN)).astype(bf16)

    deal(add2, got2, t_send, t_recv)

    @pl.when(worker)
    def _():
        def step(k, s):
            i = n_row - 1 - k
            s_low = s.astype(bf16)
            kept = s - dot(s_low, loss_turned[i], NN)
            sent2[i] = s_low
            give_back(i, sent2, grad, u_send, u_recv)
            landed(got2.at[i], t_recv.at[i])
            return kept + got2[i].astype(f32)

        lax.fori_loop(0, n_row, step, jnp.zeros((16, 128), f32), unroll=UNROLL)
        grad[a, lane_rows, :] = sent2[me]

    landed(grad.at[pl.ds(0, 2)], u_recv)

    n = 128
    rows_i = lax.broadcasted_iota(jnp.int32, (n, n), 0)
    cols_i = lax.broadcasted_iota(jnp.int32, (n, n), 1)
    own_tokens = pl.ds(pl.multiple_of(a * 128, 128), 128)
    later = []
    for h in range(2):
        p = slice(h * 128, (h + 1) * 128)
        c = cols[h]
        rs, tail, b = c[:, 0:1], c[:, 2:3], c[:, 3:4]
        d_u = summed[h] + (tail * rs) * dot(x_ref[:, p], grad[h], NT)
        grown = dot_both(inv[h], d_u, TN)
        later.append(grown)
        dv_all[own_tokens, p] = (b * grown).astype(bf16)
    mine = dv_all.at[own_tokens, :]
    remote(mine, mine, dv_sem.at[0], dv_sem.at[1], other, col)

    def query_key_grads(h):
        p = slice(h * 128, (h + 1) * 128)
        q, x = q_ref[:, p], x_ref[:, p]
        c = cols[h]
        rs, decay, tail, b = c[:, 0:1], c[:, 1:2], c[:, 2:3], c[:, 3:4]
        s, g, u, d_raw, grown = state[h], grad[h], fresh[h], grad_raw[h], later[h]
        rs_row = jnp.sum(jnp.where(rows_i == cols_i, rs, 0.0), axis=0, keepdims=True)
        d_read = dot_both(d_raw, u, NT) * within[h]
        dq_ref[:, p] = (decay * dot_left(d_raw, s, NN) + dot_left(d_read * rs_row, x, NN)).astype(bf16)
        d_gram = jnp.where(rows_i > cols_i, -b * within[h] * dot_both(grown, u, NT), 0.0)
        d_k = (
            dot_left(d_read, q, TN)
            + tail * dot_left(u, g, NN)
            - (b * decay) * dot_left(grown, s, NN)
            + dot_left(d_gram * rs_row, x, NN)
            + dot_left(d_gram * rs, x, TN)
        )
        unit = rs * x.astype(f32)
        dk_ref[:, p] = (rs * (d_k - unit * jnp.sum(unit * d_k, axis=1, keepdims=True))).astype(bf16)

    their_tokens = pl.ds(pl.multiple_of((1 - a) * 128, 128), 128)
    theirs = dv_all.at[their_tokens, :]
    early = [
        dot(act_all[a, d // 2, d % 2], dv_all[own_tokens, :], TN)
        for d in ((z + 8) % n_z, (z + n_z - 7) % n_z)
    ]
    landed(theirs, dv_sem.at[1])

    def w_term(d):
        acc = dot(act_all[0, d // 2, d % 2], dv_all[0:128, :], TN)
        return acc + dot(act_all[1, d // 2, d % 2], dv_all[128:256, :], TN)

    def r_dest(s, way):
        return (z + 8 - s) % n_z if way == 0 else (z + n_z - 7 + s) % n_z

    def r_slot(s, way):
        return w_right.at[s] if way == 0 else w_left.at[s]

    def r_send(s, way):
        d = r_dest(s, way)
        for sub in range(R_SUBS):
            q = pl.ds(sub * R_SUB, R_SUB)
            if s > 0:
                landed(r_slot(s - 1, way).at[q, :], r_sem.at[way, s - 1, sub])
                w_terms[d, q, :] = (
                    w_terms[d, q, :].astype(f32) + r_slot(s - 1, way)[q, :].astype(f32)
                ).astype(bf16)
            remote(w_terms.at[d, q, :], r_slot(s, way).at[q, :], r_sent, r_sem.at[way, s, sub],
                   up if way == 0 else down, col)

    def r_make(s):
        for way in range(2):
            if way == 1 and s == 7:
                continue
            d = r_dest(s, way)
            w_terms[d] = w_term(d).astype(bf16)

    def r_step(s):
        for way in range(2):
            if way == 1 and s == 7:
                continue
            r_send(s, way)

    def in_make(cc):
        for i in range(2):
            both = dot(dv_all[...], w_all[cc * 2 + i], NT).astype(bf16)
            for t in range(2):
                in_terms[t, cc, i] = both[t * 128 : (t + 1) * 128]

    def plus(t, cc, f, ref):
        in_terms[t, cc, f] = (in_terms[t, cc, f].astype(f32) + ref[...].astype(f32)).astype(bf16)

    def sib_send(k):
        cc = k * 2 + 1 - core
        in_make(cc)
        for t in range(2):
            for f in range(2):
                remote(in_terms.at[t, cc, f], in_sib.at[t, k, f], i_sent, sib_sem.at[t, k, f], me, twin)

    def own_make(k):
        in_make(k * 2 + core)

    def near_send(i):
        t, xh, f = i // 4, (i // 2) % 2, i % 2
        k = (1 - first) * 2 + xh
        cc = k * 2 + core
        landed(in_sib.at[t, k, f], sib_sem.at[t, k, f])
        plus(t, cc, f, in_sib.at[t, k, f])
        remote(in_terms.at[t, cc, f], in_near.at[t, xh, f], i_sent, near_sem.at[t, xh, f], me, col_near)

    def far_send(i):
        t, xh, f = i // 4, (i // 2) % 2, i % 2
        k = first * 2 + xh
        cc = k * 2 + core
        landed(in_sib.at[t, k, f], sib_sem.at[t, k, f])
        plus(t, cc, f, in_sib.at[t, k, f])
        landed(in_near.at[t, xh, f], near_sem.at[t, xh, f])
        plus(t, cc, f, in_near.at[t, xh, f])

        @pl.when(jnp.logical_not(source))
        def _():
            remote(in_terms.at[t, cc, f], in_far.at[t, xh, f], i_sent, far_sem.at[t, xh, f], me, col_far)

    def home_send(i):
        t, xh, f = i // 4, (i // 2) % 2, i % 2
        k = first * 2 + xh
        cc = k * 2 + core

        @pl.when(source)
        def _():
            landed(in_far.at[t, xh, f], far_sem.at[t, xh, f])
            plus(t, cc, f, in_far.at[t, xh, f])
            row_to, col_to = t * n_z + z, y * 4 + xh * 2 + core
            here = (row_to == me) & (col_to == col)
            dst, sem = in_last.at[x_hi, f], last_sem.at[x_hi, f]

            @pl.when(jnp.logical_not(here))
            def _():
                remote(in_terms.at[t, cc, f], dst, i_sent, sem, row_to, col_to)

            @pl.when(here)
            def _():
                pltpu.make_async_copy(in_terms.at[t, cc, f], dst, sem).start()

    for way in range(2):
        d = r_dest(0, way)
        term = early[way] + dot(act_all[1 - a, d // 2, d % 2], dv_all[their_tokens, :], TN)
        w_terms[d] = term.astype(bf16)
        r_send(0, way)
    for k in range(4):
        sib_send(k)
    r_make(1)
    for k in range(4):
        own_make(k)
    r_step(1)
    r_make(2)
    for i in range(4):
        near_send(i)
    r_step(2)
    for i in range(4, 8):
        near_send(i)
    r_make(3)
    query_key_grads(0)
    r_step(3)
    r_make(4)
    for i in range(4):
        far_send(i)
    r_step(4)
    r_make(5)
    for i in range(4, 8):
        far_send(i)
    query_key_grads(1)
    r_step(5)
    r_make(6)
    for i in range(4):
        home_send(i)
    r_step(6)
    r_make(7)
    for i in range(4, 8):
        home_send(i)
    r_step(7)
    own_term = w_term(z)
    for xh in range(2):
        for f in range(2):
            landed(in_last.at[xh, f], last_sem.at[xh, f])
    for i in range(2):
        din_ref[:, i * 256 : (i + 1) * 256] = (
            in_last[0, i].astype(f32) + in_last[1, i].astype(f32)
        ).astype(bf16)
    for sub in range(R_SUBS):
        q = pl.ds(sub * R_SUB, R_SUB)
        landed(w_right.at[7, q, :], r_sem.at[0, 7, sub])
        landed(w_left.at[6, q, :], r_sem.at[1, 6, sub])
    dw_ref[...] = own_term + w_right[7].astype(f32) + w_left[6].astype(f32)

    def drain(ref, count, sem):
        def one(i, _):
            pltpu.make_async_copy(ref, ref, sem).wait()
            return 0
        lax.fori_loop(0, count, one, 0)

    big = act_own.at[0]
    own = jnp.where(worker, 1, 0)
    far = jnp.where(source, 1, 0)
    self_home = jnp.where(source, 1, 0)
    drain(big, (2 - self_home + 4 + 4 * far + 8) * 2, act_sent)
    drain(w_all.at[0, pl.ds(0, SUB), :], 15 * SUBS, w_sent)
    landed(part.at[0], part_sem.at[0])
    landed(loss.at[0], loss_sent.at[0])
    drain(loss.at[0], 30, loss_sent.at[1])
    drain(got.at[0], 16 - own, s_send)
    drain(got.at[0], 16 - own, t_send)

    @pl.when(worker)
    def _():
        drain(got.at[0], n_row, b_send)
        drain(got.at[0], n_row, u_send)

    landed(mine, dv_sem.at[0])
    drain(w_all.at[0, pl.ds(0, R_SUB), :], 15 * R_SUBS, r_sent)
    drain(big, (8 + 4 + 4 * (1 - far) + (4 - 1) * far) * 2, i_sent)


def layer(act, w, q, x, og, ld, wr, gain):
    sq = (2, 128, 128)
    vm = pl.BlockSpec(memory_space=pltpu.VMEM)
    o = jax.ShapeDtypeStruct((128, 256), bf16)
    dma = pltpu.SemaphoreType.DMA
    V = pltpu.VMEM
    return pl.pallas_call(
        layer_kernel,
        out_shape=(
            o,
            jax.ShapeDtypeStruct((128, 512), bf16),
            o,
            o,
            jax.ShapeDtypeStruct((256, 256), f32),
        ),
        in_specs=[pl.BlockSpec(memory_space=pltpu.HBM)] * 8,
        out_specs=(vm,) * 5,
        scratch_shapes=[
            V(sq, f32), V(sq, f32), V(sq, f32), V(sq, f32), V(sq, f32), V(sq, bf16),
            V(sq, f32), V(sq, f32), V(sq, f32), V((128, 256), bf16),
            V((2, 128, 256), bf16), V((2, 8, 2, 128, 256), bf16), V((16, 256, 256), bf16),
            V((2, 128, 256), f32), V((128, 256), f32), V((16, 2, 128, 128), bf16),
            V(sq, bf16), V(sq, bf16), V((32, 16, 128), bf16), V((32, 16, 128), bf16),
            V((32, 16, 128), bf16), V((32, 16, 128), bf16), V((3, 128, 128), bf16), V((3, 128, 128), bf16),
            V((256, 256), bf16), V((16, 256, 256), bf16), V((8, 256, 256), bf16),
            V((7, 256, 256), bf16), V((2, 8, 2, 128, 256), bf16), V((2, 4, 2, 128, 256), bf16),
            V((2, 2, 2, 128, 256), bf16), V((2, 2, 2, 128, 256), bf16), V((2, 2, 128, 256), bf16),
            dma((2, 8, 2)), dma, dma((2, 8, SUBS)), dma, dma((2,)), dma((3, 8, 2)), dma((2,)),
            dma, dma((32,)), dma, dma, dma, dma((32,)), dma, dma,
            dma((2,)), dma((2, 8, R_SUBS)), dma, dma, dma((2, 4, 2)), dma((2, 2, 2)), dma((2, 2, 2)), dma((2, 2)),
            V((128, 256), bf16), V((128, 256), bf16), V((128, 256), bf16), V((2, 128), f32),
            V((2, 128), f32), V((1, 128), f32), dma((9,)), V((32, 128, 128), bf16),
        ],
        compiler_params=pltpu.CompilerParams(
            collective_id=1, has_side_effects=True, vmem_limit_bytes=63 * 1024 * 1024
        ),
        name="layer",
    )(act, w, q, x, og, ld, wr, gain)


def finish_kernel(*refs):
    for src, dst in zip(refs[:5], refs[5:]):
        dst[...] = src[...]


def finished(results):
    return pl.pallas_call(
        finish_kernel,
        out_shape=tuple(jax.ShapeDtypeStruct(r.shape, r.dtype) for r in results),
        name="finish",
    )(*results)


def shards(
    activations, w_value, query_input, key_input, log_decay, write_rate, norm_gain, out_grad
):
    return finished(layer(
        activations, w_value, query_input, key_input, out_grad, log_decay, write_rate,
        norm_gain.reshape(1, -1),
    ))


def solution(mesh):
    split = P("row", "col")
    flipped = P("col", "row")
    return jax.shard_map(
        shards,
        mesh=mesh,
        in_specs=(split, split, split, split, flipped, flipped, P(), split),
        out_specs=(split,) * 5,
        check_vma=False,
    )
```
